256 devices in a mesh: seq: 64 (over x, y, z_hi), head: 4 (over z_lo, core).
Axes of the slice: x: 4, y: 4, z: 8 (z_hi: 4, z_lo: 2; z = z_hi * 2 + z_lo), core: 2. Of those that a mesh axis runs over, the one named last changes fastest.
Arguments:
- trunk_keys: bfloat16 [4, 32768, 512], P('head', 'seq'), may hold values from -6 to 6
- trunk_values: bfloat16 [4, 32768, 512], P('head', 'seq'), may hold values from -6 to 6
- trunk_rates: float32 [4, 32768], P('head', 'seq'), may hold values from 0.001 to 0.01
- segment_end: int32 [1], replicated, may hold values from 8192 to 24576
- fast_weights: bfloat16 [3, 4, 512, 512], P(None, 'head'), may hold values from -0.25 to 0.25
- step_sizes: float32 [4], P('head'), may hold values from 0.3 to 1
- branch_query: bfloat16 [4, 32768, 512], P('head', 'seq'), may hold values from -24 to 24
- branch_keys: bfloat16 [4, 32768, 512], P('head', 'seq'), may hold values from -24 to 24
- branch_values: bfloat16 [4, 32768, 512], P('head', 'seq'), may hold values from -6 to 6
- branch_lengths: int32 [16], replicated, may hold values from 1537 to 2048, as said below
- fork_points: int32 [16], replicated, may hold values from 0 to 32768
- out_gain: float32 [4, 512], P('head'), may hold values from 0.1 to 1.9
Outputs:
- branch_out: bfloat16 [4, 32768, 512], P('head', 'seq')
- fast_after: bfloat16 [3, 4, 512, 512], P(None, 'head')
The draws below stay inside these ranges and needn't reach their ends.
Inputs may be any that keep to these rules, and one draw needn't show every extreme that they name: `branch_lengths`: only the last 512 slots of a branch can be empty; some branch has all its slots live.
All inputs are finite; a program needn't handle non-finite values.
Results may differ from the reference program's by a relative error of at most 0.02.
Values may be sent and summed in bfloat16 or wider, within the bound.
No kernel may reach another device: no remote copies, remote signals or barrier semaphores. Data moves between devices by JAX's collectives and lax.ppermute only.
A program may use at most 64 MiB of HBM per device.

```python
import math
import jax
import jax.numpy as jnp
from jax import lax

HD = 512
FH = 512
NS_STEPS = 2
WIN = 512
BR_SPAN = 4
BR_DEV = 512
HEADS = 4
TRUNK = 32768
BRANCH = 32768
BRANCHES = 16
N_SEQ = 64


def base_normal(key):
    return jax.random.normal(key, (HEADS, BRANCH, HD), jnp.float32)


def draw_branch_keys(key, part):
    common = base_normal(key)
    result = jnp.clip(common, -4.0, 4.0)
    return jnp.clip(result, -24.0, 24.0).astype(jnp.bfloat16)


def draw_branch_query(key, part):
    key = jax.random.fold_in(key, 5)
    own_draw = jax.random.normal(key, (HEADS, BRANCH, HD), jnp.float32)
    result = jnp.clip(own_draw, -4.0, 4.0)
    return result.astype(jnp.bfloat16)


def draw_branch_lengths(key, part):
    key = jax.random.fold_in(key, 11)
    span_rows = BR_SPAN * BR_DEV
    lengths = jax.random.randint(key, (BRANCHES,), span_rows - BR_DEV + 1, span_rows + 1)
    full_index = jax.random.randint(jax.random.fold_in(key, 3), (), 0, BRANCHES)
    lengths = jnp.where(jnp.arange(BRANCHES, dtype=jnp.int32) == full_index, span_rows, lengths)
    return lengths.astype(jnp.int32)


def with_ends(values, key, least, high):
    longest = values.shape.index(max(values.shape))
    spots = []
    for shift in (0, 1):
        where = [jax.random.randint(jax.random.fold_in(key, axis), (), 0, length) for axis, length in enumerate(values.shape)]
        where[longest] = (where[longest] + shift) % values.shape[longest]
        spots.append(tuple(where))
    return values.at[spots[0]].set(least).at[spots[1]].set(high)


def steps_of(own_key, dims, split, smallest, largest):
    factor_of, own = 1.0, jax.random.fold_in(own_key, 6)
    for axis_at, parts in split:
        heights = jnp.exp(jax.random.uniform(jax.random.fold_in(own, axis_at), (parts,), jnp.float32, smallest / len(split), largest / len(split)))
        factor_of = factor_of * jnp.repeat(heights, dims[axis_at] // parts).reshape([-1 if axis == axis_at else 1 for axis in range(len(dims))])
    return factor_of


def bell_draw(key, dims, scale, reach, shards=(), kind=jnp.bfloat16):
    drawn = jax.random.normal(key, dims, jnp.float32) * scale
    if len(shards) > 0:
        drawn = steps_of(key, dims, shards, -0.22, 0.18) * drawn
    return jnp.clip(drawn, min=-reach, max=reach).astype(kind)


def setup_inputs(seed: int = 0) -> dict:
    key_list = jax.random.split(jax.random.key(seed), 13)
    trunk_keys = bell_draw(key_list[0], (HEADS, TRUNK, HD), 1.0, 6.0, ((0, 4), (1, 64)))
    trunk_values = bell_draw(key_list[1], (HEADS, TRUNK, HD), 1.0, 6.0, ((0, 4), (1, 64)))
    trunk_rates = jnp.clip(jnp.exp(math.log(0.01) - 2.30258502 * jax.random.uniform(key_list[2], (HEADS, TRUNK), jnp.float32) ** steps_of(key_list[2], (HEADS, TRUNK), ((0, 4), (1, 64)), -0.2, 0.2)), 0.001, 0.01)
    segment_end = jax.random.randint(key_list[3], (1,), TRUNK // 4, 3 * TRUNK // 4 + 1).astype(jnp.int32)
    fast_weights = bell_draw(key_list[4], (3, HEADS, FH, HD), HD ** -0.5, 0.25, ((1, 4),))
    step_sizes = jnp.clip(jnp.exp(math.log(1.0) - 1.2039728 * jax.random.uniform(key_list[5], (HEADS,), jnp.float32) ** steps_of(key_list[5], (HEADS,), ((0, 4),), -0.2, 0.2)), 0.3, 1.0)
    branch_query = draw_branch_query(jax.random.fold_in(key_list[12], 71), 0)
    branch_keys = draw_branch_keys(jax.random.fold_in(key_list[12], 71), 0)
    branch_values = bell_draw(key_list[8], (HEADS, BRANCH, HD), 1.0, 6.0, ((0, 4), (1, 64)))
    branch_lengths = draw_branch_lengths(jax.random.fold_in(key_list[12], 71), 0)
    fork_points = with_ends(jax.random.randint(key_list[10], (BRANCHES,), 0, TRUNK + 1), jax.random.fold_in(key_list[10], 1), 0, TRUNK).astype(jnp.int32)
    out_gain = jnp.clip(1.0 + 0.18 * jax.random.normal(key_list[11], (HEADS, HD), jnp.float32), 0.1, 1.9)
    return {"trunk_keys": trunk_keys, "trunk_values": trunk_values, "trunk_rates": trunk_rates, "segment_end": segment_end, "fast_weights": fast_weights, "step_sizes": step_sizes, "branch_query": branch_query, "branch_keys": branch_keys, "branch_values": branch_values, "branch_lengths": branch_lengths, "fork_points": fork_points, "out_gain": out_gain}


poly_one = 3.4445
poly_two = -4.775
poly_three = 2.0315

def segment_gradient(fast_state, key_rows, value_rows, rate_row):
    proj_first = jnp.dot(key_rows, fast_state[0].T, preferred_element_type=jnp.float32)
    proj_third = jnp.dot(key_rows, fast_state[1].T, preferred_element_type=jnp.float32)
    sigmoid_first = jax.nn.sigmoid(proj_first)
    silu_first = proj_first * sigmoid_first
    hidden = (silu_first * proj_third).astype(jnp.bfloat16)
    pushed = (rate_row[:, None] * value_rows.astype(jnp.float32)).astype(jnp.bfloat16)
    returned = jnp.dot(pushed, fast_state[2].T, preferred_element_type=jnp.float32)
    delta_first = (returned * proj_third * sigmoid_first * (1.0 + proj_first * (1.0 - sigmoid_first))).astype(jnp.bfloat16)
    delta_third = (returned * silu_first).astype(jnp.bfloat16)
    grad_first = jnp.dot(delta_first.T, key_rows, preferred_element_type=jnp.float32)
    grad_third = jnp.dot(delta_third.T, key_rows, preferred_element_type=jnp.float32)
    grad_second = jnp.dot(hidden.T, pushed, preferred_element_type=jnp.float32)
    return jnp.stack([grad_first, grad_third, grad_second])

def orthogonalize(summed):
    frobenius = jnp.sqrt(lax.optimization_barrier(jnp.sum(summed * summed, axis=(-2, -1), keepdims=True)))
    current = (summed / (frobenius + 1e-07)).astype(jnp.bfloat16)
    highest = lax.Precision.HIGHEST
    for sweep_index in range(NS_STEPS):
        wide_copy = current.astype(jnp.float32)
        gram_matrix = jnp.einsum('...ij,...kj->...ik', wide_copy, wide_copy, precision=highest).astype(jnp.bfloat16)
        gram_wide = gram_matrix.astype(jnp.float32)
        square = jnp.einsum('...ij,...jk->...ik', gram_wide, gram_wide, precision=highest)
        polynomial = (poly_two * gram_wide + poly_three * square).astype(jnp.bfloat16)
        update_term = jnp.einsum('...ij,...jk->...ik', polynomial.astype(jnp.float32), wide_copy, precision=highest)
        current = (poly_one * wide_copy + update_term).astype(jnp.bfloat16)
    return current

def refresh(weights, direction, step_sizes):
    old_rows = weights.astype(jnp.float32)
    moved_rows = old_rows + step_sizes[:, None, None, None] * direction.astype(jnp.float32)
    old_scale = jnp.sqrt(lax.optimization_barrier(jnp.mean(old_rows * old_rows, axis=-1, keepdims=True)) + 1e-06)
    new_scale = jnp.sqrt(lax.optimization_barrier(jnp.mean(moved_rows * moved_rows, axis=-1, keepdims=True)) + 1e-06)
    return (moved_rows * (old_scale / new_scale)).astype(jnp.bfloat16)

def reference(trunk_keys, trunk_values, trunk_rates, segment_end, fast_weights, step_sizes, branch_query, branch_keys, branch_values, branch_lengths, fork_points, out_gain):
    split_point = segment_end[0]
    positions = jnp.arange(TRUNK, dtype=jnp.int32)
    weights = jnp.moveaxis(fast_weights, 1, 0)
    states = [weights]
    for period in range(2):
        inside = positions < split_point if period == 0 else positions >= split_point
        masked = trunk_rates * inside.astype(jnp.float32)[None, :]
        summed = lax.map(lambda packed_item: segment_gradient(*packed_item), (weights, trunk_keys, trunk_values, masked))
        direction = orthogonalize(summed)
        weights = refresh(weights, direction, step_sizes)
        states.append(weights)
    stacked = jnp.stack(states)
    chosen = jnp.where(fork_points < split_point, 0, jnp.where(fork_points < TRUNK, 1, 2)).astype(jnp.int32)
    scale = HD ** (-0.5)

    def branch_block(block_index):
        branch_id = (block_index // BR_SPAN).astype(jnp.int32)
        span_pos = (block_index % BR_SPAN).astype(jnp.int32)
        start_row = (block_index * BR_DEV).astype(jnp.int32)
        query_rows = lax.dynamic_slice_in_dim(branch_query, start_row, BR_DEV, 1).astype(jnp.float32)
        own_keys = lax.dynamic_slice_in_dim(branch_keys, start_row, BR_DEV, 1)
        own_values = lax.dynamic_slice_in_dim(branch_values, start_row, BR_DEV, 1)
        prior_start = jnp.maximum(start_row - WIN, 0).astype(jnp.int32)
        prior_keys = lax.dynamic_slice_in_dim(branch_keys, prior_start, WIN, 1)
        prior_values = lax.dynamic_slice_in_dim(branch_values, prior_start, WIN, 1)
        length_here = jnp.clip(branch_lengths[branch_id] - span_pos * BR_DEV, 0, BR_DEV)
        all_keys = jnp.concatenate([prior_keys, own_keys], axis=1).astype(jnp.float32)
        all_values = jnp.concatenate([prior_values, own_values], axis=1).astype(jnp.float32)
        slot_index = jnp.arange(WIN + BR_DEV, dtype=jnp.int32)
        live_slots = jnp.where(slot_index < WIN, span_pos > 0, slot_index - WIN < length_here)
        row_index = jnp.arange(BR_DEV, dtype=jnp.int32)[:, None]
        allowed = (slot_index[None, :] == row_index + WIN) | live_slots[None, :] & (slot_index[None, :] > row_index) & (slot_index[None, :] <= row_index + WIN)
        scores = jnp.einsum('hrd,hkd->hrk', query_rows, all_keys) * scale
        scores = jnp.where(allowed[None], scores, -jnp.inf)
        row_max = lax.optimization_barrier(jnp.max(scores, axis=-1, keepdims=True))
        exponent = jnp.exp(scores - row_max)
        attention_weights = (exponent / lax.optimization_barrier(jnp.sum(exponent, axis=-1, keepdims=True))).astype(jnp.bfloat16)
        attended = jnp.einsum('hrk,hkd->hrd', attention_weights.astype(jnp.float32), all_values)
        fast_set = jnp.take(stacked, chosen[branch_id], axis=0).astype(jnp.float32)
        proj_first = jnp.einsum('hrd,hfd->hrf', query_rows, fast_set[:, 0])
        proj_third = jnp.einsum('hrd,hfd->hrf', query_rows, fast_set[:, 1])
        hidden = (jax.nn.silu(proj_first) * proj_third).astype(jnp.bfloat16)
        applied = jnp.einsum('hrf,hfd->hrd', hidden.astype(jnp.float32), fast_set[:, 2])
        summed = attended + applied
        energy = lax.optimization_barrier(jnp.sum(summed * summed, axis=(0, 2))) / (HEADS * HD)
        normed = summed * lax.rsqrt(energy + 1e-06)[None, :, None] * out_gain[:, None, :]
        result = jnp.where((row_index[:, 0] < length_here)[None, :, None], normed, 0.0)
        return result.astype(jnp.bfloat16)
    blocks = lax.map(branch_block, jnp.arange(N_SEQ, dtype=jnp.int32))
    branch_out = jnp.moveaxis(blocks, 0, 1).reshape(HEADS, BRANCH, HD)
    return (branch_out, jnp.moveaxis(weights, 0, 1))
```

```python
import jax
import jax.numpy as jnp
from jax import lax
from jax.sharding import Mesh
from jax.sharding import PartitionSpec as P

NS_STEPS = 2
WIN = 512
BR_SPAN = 4


poly_one = 3.4445
poly_two = -4.775
poly_three = 2.0315


PLANE = ("x", "y")
SEQ = ("x", "y", "z")
HEAD = ("w", "c")


def from_behind(value):
    count = lax.axis_size("z")
    return lax.ppermute(value, "z", [(source, source + 1) for source in range(count - 1)])


def sum_everywhere(partial_sums):
    kinds, rows, columns = partial_sums.shape
    planes = lax.axis_size(PLANE)
    depth = lax.axis_size("z")
    parts = partial_sums.astype(jnp.bfloat16).reshape(kinds, planes, rows // planes, columns)
    received = lax.all_to_all(parts.swapaxes(0, 1), PLANE, 0, 0, tiled=False)
    mine = jnp.sum(received.astype(jnp.float32), axis=0).astype(jnp.bfloat16)
    total = mine.astype(jnp.float32)
    for step in range(1, depth):
        other = lax.ppermute(mine, "z", [(i, (i + step) % depth) for i in range(depth)])
        total = total + other.astype(jnp.float32)
    total = total.astype(jnp.bfloat16)
    return lax.all_to_all(
        jnp.broadcast_to(total[None], (planes, *total.shape)), PLANE, 0, 0, tiled=False
    )


def segment_gradient(fast_state, key_rows, value_rows, rate_row):
    proj_first = jnp.dot(key_rows, fast_state[0].T, preferred_element_type=jnp.float32)
    proj_third = jnp.dot(key_rows, fast_state[1].T, preferred_element_type=jnp.float32)
    sigmoid_first = jax.nn.sigmoid(proj_first)
    silu_first = proj_first * sigmoid_first
    hidden = (silu_first * proj_third).astype(jnp.bfloat16)
    pushed = (rate_row[:, None] * value_rows.astype(jnp.float32)).astype(jnp.bfloat16)
    returned = jnp.dot(pushed, fast_state[2].T, preferred_element_type=jnp.float32)
    delta_first = (
        returned * proj_third * sigmoid_first * (1.0 + proj_first * (1.0 - sigmoid_first))
    ).astype(jnp.bfloat16)
    delta_third = (returned * silu_first).astype(jnp.bfloat16)
    contract = (((0,), (0,)), ((), ()))
    grad_first = lax.dot_general(
        delta_first, key_rows, contract, preferred_element_type=jnp.float32
    )
    grad_third = lax.dot_general(
        delta_third, key_rows, contract, preferred_element_type=jnp.float32
    )
    grad_second = lax.dot_general(hidden, pushed, contract, preferred_element_type=jnp.float32)
    return jnp.stack([grad_first, grad_third, grad_second])


def normalize_sum(summed):
    frobenius = jnp.sqrt(jnp.sum(summed * summed, axis=(-2, -1), keepdims=True))
    return (summed / (frobenius + 1e-07)).astype(jnp.bfloat16)


def iterate_polynomial(current):
    for sweep_index in range(NS_STEPS):
        gram_matrix = jnp.einsum(
            "...ij,...kj->...ik", current, current, preferred_element_type=jnp.float32
        ).astype(jnp.bfloat16)
        square = jnp.einsum(
            "...ij,...jk->...ik", gram_matrix, gram_matrix, preferred_element_type=jnp.float32
        )
        polynomial = (poly_two * gram_matrix.astype(jnp.float32) + poly_three * square).astype(
            jnp.bfloat16
        )
        update_term = jnp.einsum(
            "...ij,...jk->...ik", polynomial, current, preferred_element_type=jnp.float32
        )
        current = (poly_one * current.astype(jnp.float32) + update_term).astype(jnp.bfloat16)
    return current


def refresh(weights, direction, step_sizes):
    old_rows = weights.astype(jnp.float32)
    moved_rows = old_rows + step_sizes[:, None, None, None] * direction.astype(jnp.float32)
    old_scale = jnp.sqrt(jnp.mean(old_rows * old_rows, axis=-1, keepdims=True) + 1e-06)
    new_scale = jnp.sqrt(jnp.mean(moved_rows * moved_rows, axis=-1, keepdims=True) + 1e-06)
    return (moved_rows * (old_scale / new_scale)).astype(jnp.bfloat16)


def per_device(
    trunk_keys,
    trunk_values,
    trunk_rates,
    segment_end,
    fast_weights,
    step_sizes,
    branch_query,
    branch_keys,
    branch_values,
    branch_lengths,
    fork_points,
    out_gain,
):
    prior_keys, prior_values = from_behind((branch_keys, branch_values))
    seq_count = lax.axis_size(SEQ)
    seq_index = lax.axis_index(SEQ)
    row_count = trunk_keys.shape[1]
    split_point = segment_end[0]
    positions = seq_index * row_count + jnp.arange(row_count, dtype=jnp.int32)
    weights = jnp.moveaxis(fast_weights, 1, 0)
    states = [weights]
    for period in range(2):
        inside = positions < split_point if period == 0 else positions >= split_point
        masked = trunk_rates * inside.astype(jnp.float32)[None, :]
        partial_sums = jax.vmap(segment_gradient)(weights, trunk_keys, trunk_values, masked)
        gathered = sum_everywhere(partial_sums[0])
        gathered = gathered.swapaxes(0, 1).reshape(partial_sums.shape).astype(jnp.float32)
        start_state = normalize_sum(gathered)
        direction = iterate_polynomial(start_state)
        weights = refresh(weights, direction, step_sizes)
        states.append(weights)
    head_count, branch_rows, feature_width = branch_query.shape
    all_keys = jnp.concatenate([prior_keys, branch_keys], axis=1)
    all_values = jnp.concatenate([prior_values, branch_values], axis=1)
    branch_id = seq_index // BR_SPAN
    span_pos = seq_index % BR_SPAN
    length_here = jnp.clip(
        jnp.take(branch_lengths, branch_id) - span_pos * branch_rows, 0, branch_rows
    )
    slot_index = jnp.arange(WIN + branch_rows, dtype=jnp.int32)
    live_slots = jnp.where(slot_index < WIN, span_pos > 0, slot_index - WIN < length_here)
    scale = feature_width ** (-0.5)

    def attend_block(block_index):
        start_row = block_index * WIN
        row_index = start_row + jnp.arange(WIN, dtype=jnp.int32)[:, None]
        slot_block = start_row + jnp.arange(2 * WIN, dtype=jnp.int32)[None, :]
        allowed = (slot_block == row_index + WIN) | live_slots[None, :] & (
            slot_block > row_index
        ) & (slot_block <= row_index + WIN)
        scores = (
            jnp.einsum("hrd,hkd->hrk", branch_query, all_keys, preferred_element_type=jnp.float32)
            * scale
        )
        scores = jnp.where(allowed[None], scores, -jnp.inf)
        row_max = jnp.max(scores, axis=-1, keepdims=True)
        exponent = jnp.exp(scores - row_max)
        attention_weights = (exponent / jnp.sum(exponent, axis=-1, keepdims=True)).astype(
            jnp.bfloat16
        )
        return jnp.einsum(
            "hrk,hkd->hrd", attention_weights, all_values, preferred_element_type=jnp.float32
        )

    block_count = branch_rows // WIN
    attended = lax.map(attend_block, jnp.arange(block_count, dtype=jnp.int32))
    attended = jnp.moveaxis(attended, 0, 1).reshape(head_count, branch_rows, feature_width)
    trunk_total = row_count * seq_count
    fork_here = jnp.take(fork_points, branch_id)
    chosen = jnp.where(fork_here < split_point, 0, jnp.where(fork_here < trunk_total, 1, 2))
    fast_set = jnp.take(jnp.stack(states), chosen, axis=0)
    proj_first = jnp.einsum(
        "hrd,hfd->hrf", branch_query, fast_set[:, 0], preferred_element_type=jnp.float32
    )
    proj_third = jnp.einsum(
        "hrd,hfd->hrf", branch_query, fast_set[:, 1], preferred_element_type=jnp.float32
    )
    hidden = (jax.nn.silu(proj_first) * proj_third).astype(jnp.bfloat16)
    applied = jnp.einsum("hrf,hfd->hrd", hidden, fast_set[:, 2], preferred_element_type=jnp.float32)
    summed = attended + applied
    energy = lax.psum(jnp.sum(summed * summed, axis=(0, 2)), HEAD)
    total_width = head_count * lax.axis_size(HEAD) * feature_width
    normed = summed * lax.rsqrt(energy / total_width + 1e-06)[None, :, None] * out_gain[:, None, :]
    row_index = jnp.arange(branch_rows, dtype=jnp.int32)
    result = jnp.where((row_index < length_here)[None, :, None], normed, 0.0).astype(jnp.bfloat16)
    return (result, jnp.moveaxis(weights, 0, 1))


def solution(mesh):
    fine = Mesh(mesh.devices.reshape(4, 4, 4, 2, 2), (*SEQ, *HEAD))
    rows = P(HEAD, SEQ, None)
    placed = (
        rows,
        rows,
        P(HEAD, SEQ),
        P(),
        P(None, HEAD, None, None),
        P(HEAD),
        rows,
        rows,
        rows,
        P(),
        P(),
        P(HEAD, None),
    )
    return jax.shard_map(
        per_device,
        mesh=fine,
        in_specs=placed,
        out_specs=(rows, P(None, HEAD, None, None)),
        check_vma=False,
    )
```

```python
import functools
import jax
import jax.numpy as jnp
from jax import lax
from jax.experimental import pallas as pl
from jax.experimental.pallas import tpu as pltpu
from jax.sharding import Mesh
from jax.sharding import PartitionSpec as P

PLANE = ("x", "y")
SEQ = ("x", "y", "z")
HEAD = ("w", "c")
NS_STEPS = 2
BR_SPAN = 4

poly_one = 3.4445
poly_two = -4.775
poly_three = 2.0315
VMEM_BYTES = 40 * 1024 * 1024


def nt(left, right):
    return lax.dot_general(left, right, (((1,), (1,)), ((), ())), preferred_element_type=jnp.float32)


def nn(left, right):
    return jnp.dot(left, right, preferred_element_type=jnp.float32)


def column_of(row):
    return jnp.transpose(jnp.broadcast_to(row, (128, row.shape[1])))


def emit_gradient(weights, keys_ref, values_ref, rates, parts_ref):
    planes = parts_ref.shape[0]
    step = parts_ref.shape[2]
    keys = keys_ref[...]
    rate_columns = jnp.tile(column_of(rates), (1, keys.shape[1] // 128))
    pushed = (rate_columns * values_ref[...].astype(jnp.float32)).astype(jnp.bfloat16)
    rows = weights[0].shape[0]
    chunk = 256
    for start in range(0, rows, chunk):
        cut = slice(start, start + chunk)
        first = nt(weights[0][cut], keys)
        third = nt(weights[1][cut], keys)
        gate = jax.nn.sigmoid(first)
        silu = first * gate
        hidden = (silu * third).astype(jnp.bfloat16)
        returned = nt(weights[2][cut], pushed)
        delta_first = (returned * third * gate * (1.0 + first * (1.0 - gate))).astype(jnp.bfloat16)
        delta_third = (returned * silu).astype(jnp.bfloat16)
        for kind, grad in enumerate((nn(delta_first, keys), nn(delta_third, keys), nn(hidden, pushed))):
            grad = grad.astype(jnp.bfloat16)
            for part in range(chunk // step):
                parts_ref[start // step + part, kind] = grad[part * step : (part + 1) * step]


def emit_update(gathered_ref, weights_ref, step_size, x_ref, gram_ref, out_ref):
    planes, kinds, step, _ = gathered_ref.shape
    rows = planes * step
    for kind in range(kinds):
        wide = jnp.concatenate([gathered_ref[part, kind] for part in range(planes)], axis=0).astype(jnp.float32)
        square = jnp.sum(jnp.sum(wide * wide, axis=0, keepdims=True), axis=1, keepdims=True)
        inverse = 1.0 / (jnp.sqrt(square) + 1e-07)
        x_ref[0, kind] = (wide * inverse).astype(jnp.bfloat16)
    chunk = 256
    for sweep in range(NS_STEPS):
        now, later = sweep % 2, (sweep + 1) % 2
        for kind in range(kinds):
            full = x_ref[now, kind]
            gram_ref[kind] = nt(full, full).astype(jnp.bfloat16)
        for kind in range(kinds):
            full = x_ref[now, kind]
            gram = gram_ref[kind]
            for start in range(0, rows, chunk):
                cut = slice(start, start + chunk)
                own = gram[cut]
                poly = (poly_two * own.astype(jnp.float32) + poly_three * nn(own, gram)).astype(jnp.bfloat16)
                moved = (poly_one * full[cut].astype(jnp.float32) + nn(poly, full)).astype(jnp.bfloat16)
                if sweep < NS_STEPS - 1:
                    x_ref[later, kind, cut] = moved
                else:
                    old = weights_ref[kind, cut].astype(jnp.float32)
                    new = old + step_size * moved.astype(jnp.float32)
                    old_mean = jnp.mean(old * old, axis=-1, keepdims=True) + 1e-06
                    new_mean = jnp.mean(new * new, axis=-1, keepdims=True) + 1e-06
                    out_ref[kind, cut] = (new * (jnp.sqrt(old_mean) * lax.rsqrt(new_mean))).astype(jnp.bfloat16)


def masked_rates(rates_ref, seq_ref, split_ref, period):
    rates = rates_ref[...]
    count = rates.shape[1]
    positions = seq_ref[0] * count + lax.broadcasted_iota(jnp.int32, rates.shape, 1)
    early = positions < split_ref[0]
    return jnp.where(early if period == 0 else jnp.logical_not(early), rates, 0.0)


def first_kernel(seq_ref, split_ref, weights_ref, keys_ref, values_ref, rates_ref, parts_ref):
    rates = masked_rates(rates_ref, seq_ref, split_ref, 0)
    emit_gradient([weights_ref.at[kind] for kind in range(3)], keys_ref, values_ref, rates, parts_ref)


def second_kernel(seq_ref, split_ref, step_ref, gathered_ref, weights_ref, keys_ref, values_ref, rates_ref, state_ref, parts_ref, x_ref, gram_ref):
    emit_update(gathered_ref, weights_ref, step_ref[0], x_ref, gram_ref, state_ref)
    rates = masked_rates(rates_ref, seq_ref, split_ref, 1)
    emit_gradient([state_ref.at[kind] for kind in range(3)], keys_ref, values_ref, rates, parts_ref)


def attend_kernel(seq_ref, length_ref, query_ref, prior_keys_ref, keys_ref, prior_values_ref, values_ref, out_ref):
    rows, width = query_ref.shape
    branch = seq_ref[0] // BR_SPAN
    place = seq_ref[0] % BR_SPAN
    live = length_ref[branch] - place * rows
    scale = width ** (-0.5)
    chunk = 128
    for start in range(0, rows, chunk):
        cut = slice(start, start + chunk)
        query = query_ref[cut]
        row = start + lax.broadcasted_iota(jnp.int32, (chunk, rows), 0)
        slot = lax.broadcasted_iota(jnp.int32, (chunk, rows), 1)
        behind = slot > row
        allowed = (slot == row) | (slot < jnp.where(behind, jnp.where(place > 0, rows, 0), live))
        scores = jnp.where(behind, nt(query, prior_keys_ref[...]), nt(query, keys_ref[...])) * scale
        scores = jnp.where(allowed, scores, -1e30)
        top = jnp.max(scores, axis=-1, keepdims=True)
        power = jnp.exp(scores - top)
        share = power * (1.0 / jnp.sum(power, axis=-1, keepdims=True))
        out_ref[cut] = nn(jnp.where(behind, share, 0.0).astype(jnp.bfloat16), prior_values_ref[...]) + nn(
            jnp.where(behind, 0.0, share).astype(jnp.bfloat16), values_ref[...]
        )


def third_kernel(seq_ref, split_ref, fork_ref, step_ref, gathered_ref, weights_ref, state_ref, query_ref, attended_ref, last_ref, total_ref, energy_ref, x_ref, gram_ref, trunk_total):
    emit_update(gathered_ref, state_ref, step_ref[0], x_ref, gram_ref, last_ref)
    fork = fork_ref[seq_ref[0] // BR_SPAN]

    @pl.when(fork < split_ref[0])
    def _():
        x_ref[0] = weights_ref[...]

    @pl.when((fork >= split_ref[0]) & (fork < trunk_total))
    def _():
        x_ref[0] = state_ref[...]

    @pl.when((fork >= split_ref[0]) & (fork >= trunk_total))
    def _():
        x_ref[0] = last_ref[...]

    rows = query_ref.shape[0]
    chunk = 256
    for start in range(0, rows, chunk):
        cut = slice(start, start + chunk)
        query = query_ref[cut]
        first = nt(query, x_ref[0, 0])
        third = nt(query, x_ref[0, 1])
        hidden = (first * jax.nn.sigmoid(first) * third).astype(jnp.bfloat16)
        total = attended_ref[cut] + nn(hidden, x_ref[0, 2])
        total_ref[cut] = total
        energy = jnp.sum(total * total, axis=-1, keepdims=True)
        energy_ref[:, cut] = jnp.transpose(jnp.broadcast_to(energy, (chunk, 128)))[0:1]


def last_kernel(seq_ref, length_ref, total_ref, energy_ref, gain_ref, out_ref, width):
    rows = total_ref.shape[0]
    live = length_ref[seq_ref[0] // BR_SPAN] - (seq_ref[0] % BR_SPAN) * rows
    slot = lax.broadcasted_iota(jnp.int32, (1, rows), 1)
    inverse = jnp.where(slot < live, lax.rsqrt(energy_ref[...] / width + 1e-06), 0.0)
    columns = jnp.tile(column_of(inverse), (1, total_ref.shape[1] // 128))
    out_ref[...] = (total_ref[...] * columns * gain_ref[...]).astype(jnp.bfloat16)


SMEM = pl.BlockSpec(memory_space=pltpu.SMEM)
VMEM = pl.BlockSpec(memory_space=pltpu.VMEM)


def call(kernel, scalars, arrays, outs, scratch=(), flops=0, name=None):
    moved = sum(array.size * array.dtype.itemsize for array in (*arrays, *outs))
    return pl.pallas_call(
        kernel,
        out_shape=outs,
        in_specs=[SMEM] * len(scalars) + [VMEM] * len(arrays),
        out_specs=[VMEM] * len(outs),
        scratch_shapes=list(scratch),
        compiler_params=pltpu.CompilerParams(vmem_limit_bytes=VMEM_BYTES),
        cost_estimate=pl.CostEstimate(flops=flops, bytes_accessed=moved, transcendentals=0),
        name=name,
    )(*scalars, *arrays)


def shape(dims, kind):
    return jax.ShapeDtypeStruct(dims, kind)


def update_scratch(dims):
    return (pltpu.VMEM((2, *dims), jnp.bfloat16), pltpu.VMEM(dims, jnp.bfloat16))


def from_behind(value):
    count = lax.axis_size("z")
    return lax.ppermute(value, "z", [(source, source + 1) for source in range(count - 1)])


def sum_plane(parts):
    received = lax.all_to_all(parts, PLANE, 0, 0, tiled=False)
    return jnp.sum(received.astype(jnp.float32), axis=0).astype(jnp.bfloat16)


def sum_depth(mine):
    depth = lax.axis_size("z")
    total = mine.astype(jnp.float32)
    for step in range(1, depth):
        other = lax.ppermute(mine, "z", [(i, (i + step) % depth) for i in range(depth)])
        total = total + other.astype(jnp.float32)
    return total.astype(jnp.bfloat16)


def spread_plane(total):
    planes = lax.axis_size(PLANE)
    copies = jnp.broadcast_to(total[None], (planes, *total.shape))
    return lax.all_to_all(copies, PLANE, 0, 0, tiled=False)


def per_device(
    trunk_keys,
    trunk_values,
    trunk_rates,
    segment_end,
    fast_weights,
    step_sizes,
    branch_query,
    branch_keys,
    branch_values,
    branch_lengths,
    fork_points,
    out_gain,
):
    keys, values = trunk_keys[0], trunk_values[0]
    weights = fast_weights[:, 0]
    query, own_keys, own_values = branch_query[0], branch_keys[0], branch_values[0]
    rows, width = keys.shape
    hidden = weights.shape[1]
    planes = lax.axis_size(PLANE)
    trunk_total = rows * lax.axis_size(SEQ)
    total_width = width * lax.axis_size(HEAD)
    seq = lax.axis_index(SEQ).astype(jnp.int32).reshape(1)
    product = 2 * rows * width * hidden
    parts_shape = shape((planes, 3, hidden // planes, width), jnp.bfloat16)
    state_shape = shape(weights.shape, jnp.bfloat16)
    scratch = update_scratch(weights.shape)

    prior_keys = from_behind(own_keys)
    (parts,) = call(
        first_kernel,
        (seq, segment_end),
        (weights, keys, values, trunk_rates),
        (parts_shape,),
        flops=6 * product,
    )
    mine = sum_plane(parts)
    mine, prior_keys = lax.optimization_barrier((mine, prior_keys))
    summed, sent_values = lax.optimization_barrier((sum_depth(mine), own_values))
    prior_values = from_behind(sent_values)
    gathered, prior_values = lax.optimization_barrier((spread_plane(summed), prior_values))
    state, parts = call(
        second_kernel,
        (seq, segment_end, step_sizes),
        (gathered, weights, keys, values, trunk_rates),
        (state_shape, parts_shape),
        scratch,
        flops=24 * product,
    )
    (attended,) = call(
        attend_kernel,
        (seq, branch_lengths),
        (query, prior_keys, own_keys, prior_values, own_values),
        (shape((rows, width), jnp.float32),),
        flops=4 * product,
    )
    gathered = spread_plane(sum_depth(sum_plane(parts)))
    last, total, energy = call(
        functools.partial(third_kernel, trunk_total=trunk_total),
        (seq, segment_end, fork_points, step_sizes),
        (gathered, weights, state, query, attended),
        (state_shape, shape((rows, width), jnp.float32), shape((1, rows), jnp.float32)),
        scratch,
        flops=21 * product,
    )
    energy = lax.psum(energy, HEAD)
    (result,) = call(
        functools.partial(last_kernel, width=total_width),
        (seq, branch_lengths),
        (total, energy, out_gain),
        (shape((rows, width), jnp.bfloat16),),
    )
    return (result[None], last[:, None])


def solution(mesh):
    fine = Mesh(mesh.devices.reshape(4, 4, 4, 2, 2), (*SEQ, *HEAD))
    rows = P(HEAD, SEQ, None)
    placed = (
        rows,
        rows,
        P(HEAD, SEQ),
        P(),
        P(None, HEAD, None, None),
        P(HEAD),
        rows,
        rows,
        rows,
        P(),
        P(),
        P(HEAD, None),
    )
    return jax.shard_map(
        per_device,
        mesh=fine,
        in_specs=placed,
        out_specs=(rows, P(None, HEAD, None, None)),
        check_vma=False,
    )
```

```python
import functools
import jax
import jax.numpy as jnp
from jax import lax
from jax.experimental import pallas as pl
from jax.experimental.pallas import tpu as pltpu
from jax.sharding import Mesh
from jax.sharding import PartitionSpec as P

PLANE = ("x", "y")
SEQ = ("x", "y", "z")
HEAD = ("w", "c")
NS_STEPS = 2
BR_SPAN = 4

poly_one = 3.4445
poly_two = -4.775
poly_three = 2.0315
VMEM_BYTES = 24 * 1024 * 1024
WHOLE_VMEM = 60 * 1024 * 1024
CHUNK = 256
UPDATE_CHUNK = 512


def nt(left, right):
    return lax.dot_general(left, right, (((1,), (1,)), ((), ())), preferred_element_type=jnp.float32)


def nn(left, right):
    return jnp.dot(left, right, preferred_element_type=jnp.float32)


def column_of(row):
    return jnp.transpose(jnp.broadcast_to(row, (128, row.shape[1])))


def emit_gradient(weights, keys_ref, values_ref, rates, parts_ref, parts_hbm, sems, ready=lambda name: None):
    step = parts_ref.shape[2]
    sent = []
    rows, width = weights[0].shape
    rate_columns = jnp.tile(column_of(rates), (1, width // 128))
    ready("keys")
    keys = keys_ref[...]
    pushed = None
    for start in range(0, rows, CHUNK):
        cut = slice(start, start + CHUNK)
        if start == 0:
            ready("first")
        first = nt(weights[0][cut], keys)
        if start == 0:
            ready("third")
        third = nt(weights[1][cut], keys)
        gate = jax.nn.sigmoid(first)
        silu = first * gate
        hidden = (silu * third).astype(jnp.bfloat16)
        if start == 0:
            ready("values")
            pushed = (rate_columns * values_ref[...].astype(jnp.float32)).astype(jnp.bfloat16)
            ready("second")
        returned = nt(weights[2][cut], pushed)
        delta_first = (returned * third * gate * (1.0 + first * (1.0 - gate))).astype(jnp.bfloat16)
        delta_third = (returned * silu).astype(jnp.bfloat16)
        for kind, grad in enumerate((nn(delta_first, keys), nn(delta_third, keys), nn(hidden, pushed))):
            grad = grad.astype(jnp.bfloat16)
            for part in range(CHUNK // step):
                parts_ref[start // step + part, kind] = grad[part * step : (part + 1) * step]
            slots = pl.ds(start // step, CHUNK // step)
            copy = pltpu.make_async_copy(
                parts_ref.at[slots, kind], parts_hbm.at[slots, kind], sems.at[len(sent)]
            )
            copy.start()
            sent.append(copy)
    for copy in sent:
        copy.wait()


def fetch_gathered(gathered_hbm, gathered_ref, sems):
    copies = [
        pltpu.make_async_copy(gathered_hbm.at[:, kind], gathered_ref.at[kind], sems.at[kind])
        for kind in range(gathered_ref.shape[0])
    ]
    for copy in copies:
        copy.start()
    return copies


def emit_update(fetches, gathered_ref, old_ref, step_size, x_ref, gram_ref, out_ref, begin, ready):
    kinds, planes, step, width = gathered_ref.shape
    rows = planes * step
    for kind in range(kinds):
        fetches[kind].wait()
        wide = gathered_ref[kind].reshape(rows, width).astype(jnp.float32)
        square = jnp.sum(jnp.sum(wide * wide, axis=0, keepdims=True), axis=1, keepdims=True)
        inverse = 1.0 / (jnp.sqrt(square) + 1e-07)
        x_ref[0, kind] = (wide * inverse).astype(jnp.bfloat16)
    begin()
    for sweep in range(NS_STEPS):
        now, later = sweep % 2, (sweep + 1) % 2
        if sweep == NS_STEPS - 1:
            ready()
        for kind in range(kinds):
            full = x_ref[now, kind]
            gram_ref[kind] = nt(full, full).astype(jnp.bfloat16)
        for kind in range(kinds):
            full = x_ref[now, kind]
            gram = gram_ref[kind]
            for start in range(0, rows, UPDATE_CHUNK):
                cut = slice(start, start + UPDATE_CHUNK)
                own = gram[cut]
                poly = (poly_two * own.astype(jnp.float32) + poly_three * nn(own, gram)).astype(jnp.bfloat16)
                moved = (poly_one * full[cut].astype(jnp.float32) + nn(poly, full)).astype(jnp.bfloat16)
                if sweep < NS_STEPS - 1:
                    x_ref[later, kind, cut] = moved
                else:
                    old = old_ref[kind, cut].astype(jnp.float32)
                    new = old + step_size * moved.astype(jnp.float32)
                    old_mean = jnp.mean(old * old, axis=-1, keepdims=True) + 1e-06
                    new_mean = jnp.mean(new * new, axis=-1, keepdims=True) + 1e-06
                    out_ref[kind, cut] = (new * (jnp.sqrt(old_mean) * lax.rsqrt(new_mean))).astype(jnp.bfloat16)


def masked_rates(rates_ref, seq_ref, split_ref, period):
    rates = rates_ref[...]
    count = rates.shape[1]
    positions = seq_ref[0] * count + lax.broadcasted_iota(jnp.int32, rates.shape, 1)
    early = positions < split_ref[0]
    return jnp.where(early if period == 0 else jnp.logical_not(early), rates, 0.0)


def first_kernel(
    seq_ref,
    split_ref,
    rates_ref,
    weights_hbm,
    keys_hbm,
    values_hbm,
    parts_hbm,
    weights,
    keys,
    values,
    parts,
    sems,
    parts_sems,
):
    copies = {
        "keys": pltpu.make_async_copy(keys_hbm, keys, sems.at[0]),
        "first": pltpu.make_async_copy(weights_hbm.at[0], weights.at[0], sems.at[1]),
        "third": pltpu.make_async_copy(weights_hbm.at[1], weights.at[1], sems.at[2]),
        "values": pltpu.make_async_copy(values_hbm, values, sems.at[3]),
        "second": pltpu.make_async_copy(weights_hbm.at[2], weights.at[2], sems.at[4]),
    }
    for copy in copies.values():
        copy.start()
    rates = masked_rates(rates_ref, seq_ref, split_ref, 0)
    kinds = [weights.at[kind] for kind in range(3)]
    emit_gradient(kinds, keys, values, rates, parts, parts_hbm, parts_sems, lambda name: copies[name].wait())


def second_kernel(
    seq_ref,
    split_ref,
    step_ref,
    rates_ref,
    gathered_hbm,
    weights_hbm,
    keys_hbm,
    values_hbm,
    parts_hbm,
    state_hbm,
    weights,
    keys,
    values,
    x_ref,
    gram_ref,
    state,
    gathered,
    parts,
    sems,
    gathered_sems,
    parts_sems,
):
    fetches = fetch_gathered(gathered_hbm, gathered, gathered_sems)
    fetch_weights = pltpu.make_async_copy(weights_hbm, weights, sems.at[0])
    fetch_keys = pltpu.make_async_copy(keys_hbm, keys, sems.at[1])
    fetch_values = pltpu.make_async_copy(values_hbm, values, sems.at[2])

    def begin():
        fetch_weights.start()
        fetch_keys.start()
        fetch_values.start()

    emit_update(fetches, gathered, weights, step_ref[0], x_ref, gram_ref, state, begin, fetch_weights.wait)
    keep = pltpu.make_async_copy(state, state_hbm, sems.at[3])
    keep.start()
    rates = masked_rates(rates_ref, seq_ref, split_ref, 1)
    fetch_keys.wait()
    fetch_values.wait()
    emit_gradient([state.at[kind] for kind in range(3)], keys, values, rates, parts, parts_hbm, parts_sems)
    keep.wait()


def attend_kernel(
    seq_ref, length_ref, query_ref, keys_ref, values_ref, keys_a_ref, keys_b_ref, values_b_ref, values_c_ref, out_ref
):
    rows, width = query_ref.shape
    branch = seq_ref[0] // BR_SPAN
    place = seq_ref[0] % BR_SPAN
    live = length_ref[branch] - place * rows
    scale = width ** (-0.5)
    prior_keys = jnp.concatenate([keys_a_ref[...], keys_b_ref[...]], axis=0)
    prior_values = jnp.concatenate([values_b_ref[...], values_c_ref[...]], axis=0)
    chunk = 128
    for start in range(0, rows, chunk):
        cut = slice(start, start + chunk)
        query = query_ref[cut]
        row = start + lax.broadcasted_iota(jnp.int32, (chunk, rows), 0)
        slot = lax.broadcasted_iota(jnp.int32, (chunk, rows), 1)
        behind = slot > row
        allowed = (slot == row) | (slot < jnp.where(behind, jnp.where(place > 0, rows, 0), live))
        scores = jnp.where(behind, nt(query, prior_keys), nt(query, keys_ref[...])) * scale
        scores = jnp.where(allowed, scores, -1e30)
        top = jnp.max(scores, axis=-1, keepdims=True)
        power = jnp.exp(scores - top)
        share = power * (1.0 / jnp.sum(power, axis=-1, keepdims=True))
        out_ref[cut] = nn(jnp.where(behind, share, 0.0).astype(jnp.bfloat16), prior_values) + nn(
            jnp.where(behind, 0.0, share).astype(jnp.bfloat16), values_ref[...]
        )


def third_kernel(
    seq_ref,
    split_ref,
    fork_ref,
    step_ref,
    gathered_hbm,
    weights_hbm,
    state_hbm,
    query_hbm,
    attended_hbm,
    total_ref,
    energy_ref,
    last_hbm,
    old,
    query,
    attended,
    x_ref,
    gram_ref,
    pool,
    gathered,
    sems,
    gathered_sems,
    trunk_total,
):
    fetches = fetch_gathered(gathered_hbm, gathered, gathered_sems)
    fork = fork_ref[seq_ref[0] // BR_SPAN]
    early = fork < split_ref[0]
    final = jnp.logical_and(jnp.logical_not(early), fork >= trunk_total)
    fetch_old = pltpu.make_async_copy(state_hbm, old, sems.at[0])
    fetch_query = pltpu.make_async_copy(query_hbm, query, sems.at[1])
    fetch_attended = pltpu.make_async_copy(attended_hbm, attended, sems.at[2])
    fetch_first = pltpu.make_async_copy(weights_hbm, pool.at[1], sems.at[3])
    fetch_state = pltpu.make_async_copy(state_hbm, pool.at[1], sems.at[3])

    def begin():
        fetch_old.start()
        fetch_query.start()
        fetch_attended.start()

        @pl.when(early)
        def _():
            fetch_first.start()

        @pl.when(jnp.logical_not(early))
        def _():
            fetch_state.start()

    emit_update(fetches, gathered, old, step_ref[0], x_ref, gram_ref, pool.at[0], begin, fetch_old.wait)
    keep = pltpu.make_async_copy(pool.at[0], last_hbm, sems.at[4])
    keep.start()
    fetch_query.wait()
    fetch_attended.wait()
    fetch_state.wait()
    pick = jnp.where(final, 0, 1)
    rows = query.shape[0]
    for start in range(0, rows, UPDATE_CHUNK):
        cut = slice(start, start + UPDATE_CHUNK)
        first = nt(query[cut], pool[pick, 0])
        third = nt(query[cut], pool[pick, 1])
        hidden = (first * jax.nn.sigmoid(first) * third).astype(jnp.bfloat16)
        total = attended[cut] + nn(hidden, pool[pick, 2])
        total_ref[cut] = total
        energy = jnp.sum(total * total, axis=-1, keepdims=True)
        energy_ref[:, cut] = jnp.transpose(jnp.broadcast_to(energy, (UPDATE_CHUNK, 128)))[0:1]
    keep.wait()


def last_kernel(seq_ref, length_ref, total_ref, energy_ref, gain_ref, out_ref, width):
    rows = total_ref.shape[0]
    live = length_ref[seq_ref[0] // BR_SPAN] - (seq_ref[0] % BR_SPAN) * rows
    slot = lax.broadcasted_iota(jnp.int32, (1, rows), 1)
    inverse = jnp.where(slot < live, lax.rsqrt(energy_ref[...] / width + 1e-06), 0.0)
    columns = jnp.tile(column_of(inverse), (1, total_ref.shape[1] // 128))
    out_ref[...] = (total_ref[...] * columns * gain_ref[...]).astype(jnp.bfloat16)


def replicate_kernel(*refs):
    total = refs[0][...].astype(jnp.float32)
    for ref in refs[1:-1]:
        total = total + ref[...].astype(jnp.float32)
    total = total.astype(jnp.bfloat16)
    for slot in range(refs[-1].shape[0]):
        refs[-1][slot] = total


SMEM = pl.BlockSpec(memory_space=pltpu.SMEM)
VMEM = pl.BlockSpec(memory_space=pltpu.VMEM)
HBM = pl.BlockSpec(memory_space=pltpu.HBM)


def call(kernel, scalars, arrays, outs, held=(), held_outs=(), scratch=(), flops=0, vmem=VMEM_BYTES):
    moved = sum(array.size * array.dtype.itemsize for array in (*arrays, *held, *outs, *held_outs))
    return pl.pallas_call(
        kernel,
        out_shape=(*outs, *held_outs),
        in_specs=[SMEM] * len(scalars) + [VMEM] * len(arrays) + [HBM] * len(held),
        out_specs=[VMEM] * len(outs) + [HBM] * len(held_outs),
        scratch_shapes=list(scratch),
        compiler_params=pltpu.CompilerParams(vmem_limit_bytes=vmem),
        cost_estimate=pl.CostEstimate(flops=flops, bytes_accessed=moved, transcendentals=0),
    )(*scalars, *arrays, *held)


def shape(dims, kind):
    return jax.ShapeDtypeStruct(dims, kind)


def space(dims, kind=jnp.bfloat16):
    return pltpu.VMEM(dims, kind)


def gradient_first(seq, split, rates, weights, keys, values, parts_shape):
    scratch = (
        space(weights.shape),
        space(keys.shape),
        space(values.shape),
        space(parts_shape.shape),
        pltpu.SemaphoreType.DMA((5,)),
        pltpu.SemaphoreType.DMA((3 * keys.shape[0] // CHUNK,)),
    )
    (parts,) = call(
        first_kernel,
        (seq, split),
        (rates,),
        (),
        (weights, keys, values),
        (parts_shape,),
        scratch,
        flops=12 * keys.size * weights.shape[1],
        vmem=WHOLE_VMEM,
    )
    return parts


def by_kind(gathered):
    planes, kinds, step, width = gathered.shape
    return space((kinds, planes, step, width))


def update_and_gradient(seq, split, step, gathered, rates, weights, keys, values):
    full = weights.shape
    scratch = (
        space(full),
        space(keys.shape),
        space(values.shape),
        space((2, *full)),
        space(full),
        space(full),
        by_kind(gathered),
        space(gathered.shape),
        pltpu.SemaphoreType.DMA((4,)),
        pltpu.SemaphoreType.DMA((3,)),
        pltpu.SemaphoreType.DMA((3 * full[1] // CHUNK,)),
    )
    return call(
        second_kernel,
        (seq, split, step),
        (rates,),
        (),
        (gathered, weights, keys, values),
        (shape(gathered.shape, jnp.bfloat16), shape(full, jnp.bfloat16)),
        scratch,
        flops=48 * keys.size * full[1],
        vmem=WHOLE_VMEM,
    )


def update_and_apply(seq, split, forks, step, gathered, weights, state, query, attended, trunk_total):
    full = weights.shape
    rows, width = query.shape
    scratch = (
        space(full),
        space(query.shape),
        space(query.shape, jnp.float32),
        space((2, *full)),
        space(full),
        space((2, *full)),
        by_kind(gathered),
        pltpu.SemaphoreType.DMA((5,)),
        pltpu.SemaphoreType.DMA((3,)),
    )
    return call(
        functools.partial(third_kernel, trunk_total=trunk_total),
        (seq, split, forks, step),
        (),
        (shape((rows, width), jnp.float32), shape((1, rows), jnp.float32)),
        (gathered, weights, state, query, attended),
        (shape(full, jnp.bfloat16),),
        scratch,
        flops=42 * query.size * full[1],
        vmem=WHOLE_VMEM,
    )


def from_behind(value):
    count = lax.axis_size("z")
    return lax.ppermute(value, "z", [(source, source + 1) for source in range(count - 1)])


def sum_plane(parts):
    received = lax.all_to_all(parts, PLANE, 0, 0, tiled=False)
    return jnp.sum(received.astype(jnp.float32), axis=0).astype(jnp.bfloat16)


def sum_depth(mine):
    depth, planes = lax.axis_size("z"), lax.axis_size(PLANE)
    others = [
        lax.ppermute(mine, "z", [(i, (i + step) % depth) for i in range(depth)]) for step in range(1, depth)
    ]
    (copies,) = call(replicate_kernel, (), (mine, *others), (shape((planes, *mine.shape), mine.dtype),))
    return copies


def spread_plane(copies):
    return lax.all_to_all(copies, PLANE, 0, 0, tiled=False)


def per_device(
    trunk_keys,
    trunk_values,
    trunk_rates,
    segment_end,
    fast_weights,
    step_sizes,
    branch_query,
    branch_keys,
    branch_values,
    branch_lengths,
    fork_points,
    out_gain,
):
    keys, values = trunk_keys[0], trunk_values[0]
    weights = fast_weights[:, 0]
    query, own_keys, own_values = branch_query[0], branch_keys[0], branch_values[0]
    rows, width = keys.shape
    hidden = weights.shape[1]
    planes = lax.axis_size(PLANE)
    trunk_total = rows * lax.axis_size(SEQ)
    total_width = width * lax.axis_size(HEAD)
    seq = lax.axis_index(SEQ).astype(jnp.int32).reshape(1)
    parts_shape = shape((planes, 3, hidden // planes, width), jnp.bfloat16)
    most = 3 * rows // 4
    barrier = lax.optimization_barrier

    keys_a = from_behind(own_keys[:most])
    parts = gradient_first(seq, segment_end, trunk_rates, weights, keys, values, parts_shape)
    mine, keys_a = barrier((sum_plane(parts), keys_a))
    copies, rest_keys, rest_values = barrier((sum_depth(mine), own_keys[most:], own_values[: rows - most]))
    gathered, keys_b, values_b = barrier((spread_plane(copies), from_behind(rest_keys), from_behind(rest_values)))
    parts, state = update_and_gradient(
        seq, segment_end, step_sizes, gathered, trunk_rates, weights, keys, values
    )
    parts, rest_values = barrier((parts, own_values[rows - most :]))
    mine, values_c = barrier((sum_plane(parts), from_behind(rest_values)))
    copies = sum_depth(mine)
    (attended,) = call(
        attend_kernel,
        (seq, branch_lengths),
        (query, own_keys, own_values, keys_a, keys_b, values_b, values_c),
        (shape((rows, width), jnp.float32),),
        flops=8 * rows * rows * width,
    )
    gathered = spread_plane(copies)
    total, energy, last = update_and_apply(
        seq, segment_end, fork_points, step_sizes, gathered, weights, state, query, attended, trunk_total
    )
    energy = lax.psum(energy, HEAD)
    (result,) = call(
        functools.partial(last_kernel, width=total_width),
        (seq, branch_lengths),
        (total, energy, out_gain),
        (shape((rows, width), jnp.bfloat16),),
    )
    return (result[None], last[:, None])


def solution(mesh):
    fine = Mesh(mesh.devices.reshape(4, 4, 4, 2, 2), (*SEQ, *HEAD))
    rows = P(HEAD, SEQ, None)
    placed = (
        rows,
        rows,
        P(HEAD, SEQ),
        P(),
        P(None, HEAD, None, None),
        P(HEAD),
        rows,
        rows,
        rows,
        P(),
        P(),
        P(HEAD, None),
    )
    return jax.shard_map(
        per_device,
        mesh=fine,
        in_specs=placed,
        out_specs=(rows, P(None, HEAD, None, None)),
        check_vma=False,
    )
```

```python
import functools
import jax
import jax.numpy as jnp
from jax import lax
from jax.experimental import pallas as pl
from jax.experimental.pallas import tpu as pltpu
from jax.sharding import Mesh
from jax.sharding import PartitionSpec as P

PLANE = ("x", "y")
SEQ = ("x", "y", "z")
HEAD = ("w", "c")
NS_STEPS = 2
BR_SPAN = 4

poly_one = 3.4445
poly_two = -4.775
poly_three = 2.0315
VMEM_BYTES = 24 * 1024 * 1024
WHOLE_VMEM = 60 * 1024 * 1024
LAST_VMEM = 50 * 1024 * 1024
SECOND_VMEM = 60 * 1024 * 1024
CHUNK = 256
UPDATE_CHUNK = 512


def nt(left, right):
    return lax.dot_general(left, right, (((1,), (1,)), ((), ())), preferred_element_type=jnp.float32)


def nn(left, right):
    return jnp.dot(left, right, preferred_element_type=jnp.float32)


def column_of(row):
    return jnp.transpose(jnp.broadcast_to(row, (128, row.shape[1])))


def emit_gradient(weights, keys_ref, values_ref, rates, parts_ref, parts_hbm, sems, ready=lambda name: None):
    step = parts_ref.shape[2]
    sent = []
    rows, width = weights[0].shape
    rate_columns = jnp.tile(column_of(rates), (1, width // 128))
    ready("keys")
    keys = keys_ref[...]
    pushed = None
    for start in range(0, rows, CHUNK):
        cut = slice(start, start + CHUNK)
        if start == 0:
            ready("first")
        first = nt(weights[0][cut], keys)
        if start == 0:
            ready("third")
        third = nt(weights[1][cut], keys)
        gate = jax.nn.sigmoid(first)
        silu = first * gate
        hidden = (silu * third).astype(jnp.bfloat16)
        if start == 0:
            ready("values")
            pushed = (rate_columns * values_ref[...].astype(jnp.float32)).astype(jnp.bfloat16)
            ready("second")
        returned = nt(weights[2][cut], pushed)
        delta_first = (returned * third * gate * (1.0 + first * (1.0 - gate))).astype(jnp.bfloat16)
        delta_third = (returned * silu).astype(jnp.bfloat16)
        for kind, grad in enumerate((nn(delta_first, keys), nn(delta_third, keys), nn(hidden, pushed))):
            grad = grad.astype(jnp.bfloat16)
            for part in range(CHUNK // step):
                parts_ref[start // step + part, kind] = grad[part * step : (part + 1) * step]
            slots = pl.ds(start // step, CHUNK // step)
            copy = pltpu.make_async_copy(
                parts_ref.at[slots, kind], parts_hbm.at[slots, kind], sems.at[len(sent)]
            )
            copy.start()
            sent.append(copy)
    for copy in sent:
        copy.wait()


def fetch_gathered(gathered_hbm, gathered_ref, sems):
    copies = [
        pltpu.make_async_copy(gathered_hbm.at[:, kind], gathered_ref.at[kind], sems.at[kind])
        for kind in range(gathered_ref.shape[0])
    ]
    for copy in copies:
        copy.start()
    return copies


def emit_update(fetches, gathered_ref, old_ref, step_size, x_ref, gram_ref, out_ref, begin, ready):
    kinds, planes, step, width = gathered_ref.shape
    rows = planes * step
    for kind in range(kinds):
        fetches[kind].wait()
        wide = gathered_ref[kind].reshape(rows, width).astype(jnp.float32)
        square = jnp.sum(jnp.sum(wide * wide, axis=0, keepdims=True), axis=1, keepdims=True)
        inverse = 1.0 / (jnp.sqrt(square) + 1e-07)
        x_ref[0, kind] = (wide * inverse).astype(jnp.bfloat16)
    begin()
    for sweep in range(NS_STEPS):
        now, later = sweep % 2, (sweep + 1) % 2
        if sweep == NS_STEPS - 1:
            ready()
        for kind in range(kinds):
            full = x_ref[now, kind]
            gram_ref[kind] = nt(full, full).astype(jnp.bfloat16)
        for kind in range(kinds):
            full = x_ref[now, kind]
            gram = gram_ref[kind]
            for start in range(0, rows, UPDATE_CHUNK):
                cut = slice(start, start + UPDATE_CHUNK)
                own = gram[cut]
                poly = (poly_two * own.astype(jnp.float32) + poly_three * nn(own, gram)).astype(jnp.bfloat16)
                moved = (poly_one * full[cut].astype(jnp.float32) + nn(poly, full)).astype(jnp.bfloat16)
                if sweep < NS_STEPS - 1:
                    x_ref[later, kind, cut] = moved
                else:
                    old = old_ref[kind, cut].astype(jnp.float32)
                    new = old + step_size * moved.astype(jnp.float32)
                    old_mean = jnp.mean(old * old, axis=-1, keepdims=True) + 1e-06
                    new_mean = jnp.mean(new * new, axis=-1, keepdims=True) + 1e-06
                    out_ref[kind, cut] = (new * (jnp.sqrt(old_mean) * lax.rsqrt(new_mean))).astype(jnp.bfloat16)


def masked_rates(rates_ref, seq_ref, split_ref, period):
    rates = rates_ref[...]
    count = rates.shape[1]
    positions = seq_ref[0] * count + lax.broadcasted_iota(jnp.int32, rates.shape, 1)
    early = positions < split_ref[0]
    return jnp.where(early if period == 0 else jnp.logical_not(early), rates, 0.0)


def first_kernel(
    seq_ref,
    split_ref,
    rates_ref,
    weights_hbm,
    keys_hbm,
    values_hbm,
    parts_hbm,
    weights,
    keys,
    values,
    parts,
    sems,
    parts_sems,
):
    copies = {
        "keys": pltpu.make_async_copy(keys_hbm, keys, sems.at[0]),
        "first": pltpu.make_async_copy(weights_hbm.at[0], weights.at[0], sems.at[1]),
        "third": pltpu.make_async_copy(weights_hbm.at[1], weights.at[1], sems.at[2]),
        "values": pltpu.make_async_copy(values_hbm, values, sems.at[3]),
        "second": pltpu.make_async_copy(weights_hbm.at[2], weights.at[2], sems.at[4]),
    }
    for copy in copies.values():
        copy.start()
    rates = masked_rates(rates_ref, seq_ref, split_ref, 0)
    kinds = [weights.at[kind] for kind in range(3)]
    emit_gradient(kinds, keys, values, rates, parts, parts_hbm, parts_sems, lambda name: copies[name].wait())


def second_kernel(
    seq_ref,
    split_ref,
    step_ref,
    rates_ref,
    gathered_hbm,
    weights_hbm,
    keys_hbm,
    values_hbm,
    parts_hbm,
    state_hbm,
    weights,
    keys,
    values,
    x_ref,
    gram_ref,
    state,
    gathered,
    parts,
    sems,
    gathered_sems,
    parts_sems,
):
    fetches = fetch_gathered(gathered_hbm, gathered, gathered_sems)
    fetch_weights = pltpu.make_async_copy(weights_hbm, weights, sems.at[0])
    fetch_keys = pltpu.make_async_copy(keys_hbm, keys, sems.at[1])
    fetch_values = pltpu.make_async_copy(values_hbm, values, sems.at[2])

    def begin():
        fetch_weights.start()
        fetch_keys.start()
        fetch_values.start()

    emit_update(fetches, gathered, weights, step_ref[0], x_ref, gram_ref, state, begin, fetch_weights.wait)
    keep = pltpu.make_async_copy(state, state_hbm, sems.at[3])
    keep.start()
    rates = masked_rates(rates_ref, seq_ref, split_ref, 1)
    fetch_keys.wait()
    fetch_values.wait()
    emit_gradient([state.at[kind] for kind in range(3)], keys, values, rates, parts, parts_hbm, parts_sems)
    keep.wait()


def attend_kernel(
    seq_ref, length_ref, query_ref, keys_ref, values_ref, keys_a_ref, keys_b_ref, values_b_ref, values_c_ref, out_ref
):
    rows, width = query_ref.shape
    branch = seq_ref[0] // BR_SPAN
    place = seq_ref[0] % BR_SPAN
    live = length_ref[branch] - place * rows
    scale = width ** (-0.5)
    prior_keys = jnp.concatenate([keys_a_ref[...], keys_b_ref[...]], axis=0)
    prior_values = jnp.concatenate([values_b_ref[...], values_c_ref[...]], axis=0)
    chunk = 128
    for start in range(0, rows, chunk):
        cut = slice(start, start + chunk)
        query = query_ref[cut]
        row = start + lax.broadcasted_iota(jnp.int32, (chunk, rows), 0)
        slot = lax.broadcasted_iota(jnp.int32, (chunk, rows), 1)
        behind = slot > row
        allowed = (slot == row) | (slot < jnp.where(behind, jnp.where(place > 0, rows, 0), live))
        scores = jnp.where(behind, nt(query, prior_keys), nt(query, keys_ref[...])) * scale
        scores = jnp.where(allowed, scores, -1e30)
        top = jnp.max(scores, axis=-1, keepdims=True)
        power = jnp.exp(scores - top)
        share = power * (1.0 / jnp.sum(power, axis=-1, keepdims=True))
        out_ref[cut] = nn(jnp.where(behind, share, 0.0).astype(jnp.bfloat16), prior_values) + nn(
            jnp.where(behind, 0.0, share).astype(jnp.bfloat16), values_ref[...]
        )


def third_kernel(
    seq_ref,
    split_ref,
    fork_ref,
    step_ref,
    attended_ref,
    gathered_hbm,
    weights_hbm,
    state_hbm,
    query_hbm,
    total_ref,
    energy_ref,
    last_hbm,
    old,
    query,
    x_ref,
    gram_ref,
    pool,
    gathered,
    sems,
    gathered_sems,
    trunk_total,
):
    fetches = fetch_gathered(gathered_hbm, gathered, gathered_sems)
    fork = fork_ref[seq_ref[0] // BR_SPAN]
    early = fork < split_ref[0]
    final = jnp.logical_and(jnp.logical_not(early), fork >= trunk_total)
    fetch_old = pltpu.make_async_copy(state_hbm, old, sems.at[0])
    fetch_query = pltpu.make_async_copy(query_hbm, query, sems.at[1])
    fetch_first = pltpu.make_async_copy(weights_hbm, pool.at[1], sems.at[2])
    fetch_state = pltpu.make_async_copy(state_hbm, pool.at[1], sems.at[2])

    def begin():
        fetch_old.start()
        fetch_query.start()

        @pl.when(early)
        def _():
            fetch_first.start()

        @pl.when(jnp.logical_not(early))
        def _():
            fetch_state.start()

    emit_update(fetches, gathered, old, step_ref[0], x_ref, gram_ref, pool.at[0], begin, fetch_old.wait)
    keep = pltpu.make_async_copy(pool.at[0], last_hbm, sems.at[3])
    keep.start()
    fetch_query.wait()
    fetch_state.wait()
    pick = jnp.where(final, 0, 1)
    rows = query.shape[0]
    for start in range(0, rows, UPDATE_CHUNK):
        cut = slice(start, start + UPDATE_CHUNK)
        first = nt(query[cut], pool[pick, 0])
        third = nt(query[cut], pool[pick, 1])
        hidden = (first * jax.nn.sigmoid(first) * third).astype(jnp.bfloat16)
        total = attended_ref[cut] + nn(hidden, pool[pick, 2])
        total_ref[cut] = total
        energy = jnp.sum(total * total, axis=-1, keepdims=True)
        energy_ref[:, cut] = jnp.transpose(jnp.broadcast_to(energy, (UPDATE_CHUNK, 128)))[0:1]
    keep.wait()


def last_kernel(seq_ref, length_ref, total_ref, energy_ref, gain_ref, out_ref, width):
    rows = total_ref.shape[0]
    live = length_ref[seq_ref[0] // BR_SPAN] - (seq_ref[0] % BR_SPAN) * rows
    slot = lax.broadcasted_iota(jnp.int32, (1, rows), 1)
    inverse = jnp.where(slot < live, lax.rsqrt(energy_ref[...] / width + 1e-06), 0.0)
    columns = jnp.tile(column_of(inverse), (1, total_ref.shape[1] // 128))
    out_ref[...] = (total_ref[...] * columns * gain_ref[...]).astype(jnp.bfloat16)


def replicate_kernel(*refs):
    total = refs[0][...].astype(jnp.float32)
    for ref in refs[1:-1]:
        total = total + ref[...].astype(jnp.float32)
    total = total.astype(jnp.bfloat16)
    for slot in range(refs[-1].shape[0]):
        refs[-1][slot] = total


SMEM = pl.BlockSpec(memory_space=pltpu.SMEM)
VMEM = pl.BlockSpec(memory_space=pltpu.VMEM)
HBM = pl.BlockSpec(memory_space=pltpu.HBM)


def call(kernel, scalars, arrays, outs, held=(), held_outs=(), scratch=(), flops=0, vmem=VMEM_BYTES):
    moved = sum(array.size * array.dtype.itemsize for array in (*arrays, *held, *outs, *held_outs))
    return pl.pallas_call(
        kernel,
        out_shape=(*outs, *held_outs),
        in_specs=[SMEM] * len(scalars) + [VMEM] * len(arrays) + [HBM] * len(held),
        out_specs=[VMEM] * len(outs) + [HBM] * len(held_outs),
        scratch_shapes=list(scratch),
        compiler_params=pltpu.CompilerParams(vmem_limit_bytes=vmem),
        cost_estimate=pl.CostEstimate(flops=flops, bytes_accessed=moved, transcendentals=0),
    )(*scalars, *arrays, *held)


def shape(dims, kind):
    return jax.ShapeDtypeStruct(dims, kind)


def space(dims, kind=jnp.bfloat16):
    return pltpu.VMEM(dims, kind)


def gradient_first(seq, split, rates, weights, keys, values, parts_shape):
    scratch = (
        space(weights.shape),
        space(keys.shape),
        space(values.shape),
        space(parts_shape.shape),
        pltpu.SemaphoreType.DMA((5,)),
        pltpu.SemaphoreType.DMA((3 * keys.shape[0] // CHUNK,)),
    )
    (parts,) = call(
        first_kernel,
        (seq, split),
        (rates,),
        (),
        (weights, keys, values),
        (parts_shape,),
        scratch,
        flops=12 * keys.size * weights.shape[1],
        vmem=WHOLE_VMEM,
    )
    return parts


def by_kind(gathered):
    planes, kinds, step, width = gathered.shape
    return space((kinds, planes, step, width))


def update_and_gradient(seq, split, step, gathered, rates, weights, keys, values):
    full = weights.shape
    scratch = (
        space(full),
        space(keys.shape),
        space(values.shape),
        space((2, *full)),
        space(full),
        space(full),
        by_kind(gathered),
        space(gathered.shape),
        pltpu.SemaphoreType.DMA((4,)),
        pltpu.SemaphoreType.DMA((3,)),
        pltpu.SemaphoreType.DMA((3 * full[1] // CHUNK,)),
    )
    return call(
        second_kernel,
        (seq, split, step),
        (rates,),
        (),
        (gathered, weights, keys, values),
        (shape(gathered.shape, jnp.bfloat16), shape(full, jnp.bfloat16)),
        scratch,
        flops=48 * keys.size * full[1],
        vmem=SECOND_VMEM,
    )


def update_and_apply(seq, split, forks, step, gathered, weights, state, query, attended, trunk_total):
    full = weights.shape
    rows, width = query.shape
    scratch = (
        space(full),
        space(query.shape),
        space((2, *full)),
        space(full),
        space((2, *full)),
        by_kind(gathered),
        pltpu.SemaphoreType.DMA((4,)),
        pltpu.SemaphoreType.DMA((3,)),
    )
    return call(
        functools.partial(third_kernel, trunk_total=trunk_total),
        (seq, split, forks, step),
        (attended,),
        (shape((rows, width), jnp.float32), shape((1, rows), jnp.float32)),
        (gathered, weights, state, query),
        (shape(full, jnp.bfloat16),),
        scratch,
        flops=42 * query.size * full[1],
        vmem=LAST_VMEM,
    )


def from_behind(value):
    count = lax.axis_size("z")
    return lax.ppermute(value, "z", [(source, source + 1) for source in range(count - 1)])


def sum_plane(parts):
    received = lax.all_to_all(parts, PLANE, 0, 0, tiled=False)
    return jnp.sum(received.astype(jnp.float32), axis=0).astype(jnp.bfloat16)


def swap_depth(value, flip):
    depth = lax.axis_size("z")
    return lax.ppermute(value, "z", [(i, i ^ flip) for i in range(depth)])


def sum_depth(mine, beside=None):
    planes = lax.axis_size(PLANE)
    other, beside = lax.optimization_barrier((swap_depth(mine, 1), beside))
    pair = (mine.astype(jnp.float32) + other.astype(jnp.float32)).astype(jnp.bfloat16)
    (copies,) = call(
        replicate_kernel, (), (pair, swap_depth(pair, 3)), (shape((planes, *mine.shape), mine.dtype),)
    )
    return copies, beside


def spread_plane(copies):
    return lax.all_to_all(copies, PLANE, 0, 0, tiled=False)


def per_device(
    trunk_keys,
    trunk_values,
    trunk_rates,
    segment_end,
    fast_weights,
    step_sizes,
    branch_query,
    branch_keys,
    branch_values,
    branch_lengths,
    fork_points,
    out_gain,
):
    keys, values = trunk_keys[0], trunk_values[0]
    weights = fast_weights[:, 0]
    query, own_keys, own_values = branch_query[0], branch_keys[0], branch_values[0]
    rows, width = keys.shape
    hidden = weights.shape[1]
    planes = lax.axis_size(PLANE)
    trunk_total = rows * lax.axis_size(SEQ)
    total_width = width * lax.axis_size(HEAD)
    seq = lax.axis_index(SEQ).astype(jnp.int32).reshape(1)
    parts_shape = shape((planes, 3, hidden // planes, width), jnp.bfloat16)
    barrier = lax.optimization_barrier
    most = 3 * rows // 4

    keys_a = from_behind(own_keys[:most])
    parts = gradient_first(seq, segment_end, trunk_rates, weights, keys, values, parts_shape)
    mine, keys_a = barrier((sum_plane(parts), keys_a))
    copies, _ = sum_depth(mine)
    copies, rest_keys, rest_values = barrier((copies, own_keys[most:], own_values[: rows - most]))
    gathered, keys_b, values_b = barrier((spread_plane(copies), from_behind(rest_keys), from_behind(rest_values)))
    parts, state = update_and_gradient(
        seq, segment_end, step_sizes, gathered, trunk_rates, weights, keys, values
    )
    parts, rest_values = barrier((parts, own_values[rows - most :]))
    mine, values_c, query = barrier((sum_plane(parts), from_behind(rest_values), query))
    (attended,) = call(
        attend_kernel,
        (seq, branch_lengths),
        (query, own_keys, own_values, keys_a, keys_b, values_b, values_c),
        (shape((rows, width), jnp.float32),),
        flops=8 * rows * rows * width,
    )
    copies, attended = sum_depth(mine, attended)
    gathered = spread_plane(copies)
    total, energy, last = update_and_apply(
        seq, segment_end, fork_points, step_sizes, gathered, weights, state, query, attended, trunk_total
    )
    energy = lax.psum(energy, HEAD)
    (result,) = call(
        functools.partial(last_kernel, width=total_width),
        (seq, branch_lengths),
        (total, energy, out_gain),
        (shape((rows, width), jnp.bfloat16),),
    )
    return (result[None], last[:, None])


def solution(mesh):
    fine = Mesh(mesh.devices.reshape(4, 4, 4, 2, 2), (*SEQ, *HEAD))
    rows = P(HEAD, SEQ, None)
    placed = (
        rows,
        rows,
        P(HEAD, SEQ),
        P(),
        P(None, HEAD, None, None),
        P(HEAD),
        rows,
        rows,
        rows,
        P(),
        P(),
        P(HEAD, None),
    )
    return jax.shard_map(
        per_device,
        mesh=fine,
        in_specs=placed,
        out_specs=(rows, P(None, HEAD, None, None)),
        check_vma=False,
    )
```

```python
import functools
import jax
import jax.numpy as jnp
from jax import lax
from jax.experimental import pallas as pl
from jax.experimental.pallas import tpu as pltpu
from jax.sharding import Mesh
from jax.sharding import PartitionSpec as P

PLANE = ("x", "y")
SEQ = ("x", "y", "z")
HEAD = ("w", "c")
NS_STEPS = 2
BR_SPAN = 4

poly_one = 3.4445
poly_two = -4.775
poly_three = 2.0315
VMEM_BYTES = 24 * 1024 * 1024
WHOLE_VMEM = 60 * 1024 * 1024
LAST_VMEM = 46 * 1024 * 1024
SECOND_VMEM = 60 * 1024 * 1024
CHUNK = 256
UPDATE_CHUNK = 512


def nt(left, right):
    return lax.dot_general(left, right, (((1,), (1,)), ((), ())), preferred_element_type=jnp.float32)


def nn(left, right):
    return jnp.dot(left, right, preferred_element_type=jnp.float32)


def column_of(row):
    return jnp.transpose(jnp.broadcast_to(row, (128, row.shape[1])))


def emit_gradient(weights, keys_ref, values_ref, rates, parts_ref, parts_hbm, sems, ready=lambda name: None):
    step = parts_ref.shape[2]
    sent = []
    rows, width = weights[0].shape
    rate_columns = jnp.tile(column_of(rates), (1, width // 128))
    ready("keys")
    keys = keys_ref[...]
    pushed = None
    for start in range(0, rows, CHUNK):
        cut = slice(start, start + CHUNK)
        if start == 0:
            ready("first")
        first = nt(weights[0][cut], keys)
        if start == 0:
            ready("third")
        third = nt(weights[1][cut], keys)
        gate = jax.nn.sigmoid(first)
        silu = first * gate
        hidden = (silu * third).astype(jnp.bfloat16)
        if start == 0:
            ready("values")
            pushed = (rate_columns * values_ref[...].astype(jnp.float32)).astype(jnp.bfloat16)
            ready("second")
        returned = nt(weights[2][cut], pushed)
        delta_first = (returned * third * gate * (1.0 + first * (1.0 - gate))).astype(jnp.bfloat16)
        delta_third = (returned * silu).astype(jnp.bfloat16)
        for kind, grad in enumerate((nn(delta_first, keys), nn(delta_third, keys), nn(hidden, pushed))):
            grad = grad.astype(jnp.bfloat16)
            for part in range(CHUNK // step):
                parts_ref[start // step + part, kind] = grad[part * step : (part + 1) * step]
            slots = pl.ds(start // step, CHUNK // step)
            copy = pltpu.make_async_copy(
                parts_ref.at[slots, kind], parts_hbm.at[slots, kind], sems.at[len(sent)]
            )
            copy.start()
            sent.append(copy)
    for copy in sent:
        copy.wait()


def fetch_gathered(gathered_hbm, gathered_ref, sems):
    copies = [
        pltpu.make_async_copy(gathered_hbm.at[:, kind], gathered_ref.at[kind], sems.at[kind])
        for kind in range(gathered_ref.shape[0])
    ]
    for copy in copies:
        copy.start()
    return copies


def emit_update(load, old_ref, step_size, x_ref, gram_ref, out_ref, begin, ready):
    kinds, rows, width = out_ref.shape
    for kind in range(kinds):
        wide = load(kind).reshape(rows, width).astype(jnp.float32)
        square = jnp.sum(jnp.sum(wide * wide, axis=0, keepdims=True), axis=1, keepdims=True)
        inverse = 1.0 / (jnp.sqrt(square) + 1e-07)
        x_ref[0, kind] = (wide * inverse).astype(jnp.bfloat16)
    begin()
    for sweep in range(NS_STEPS):
        now, later = sweep % 2, (sweep + 1) % 2
        if sweep == NS_STEPS - 1:
            ready()
        for kind in range(kinds):
            full = x_ref[now, kind]
            gram_ref[kind] = nt(full, full).astype(jnp.bfloat16)
        for kind in range(kinds):
            full = x_ref[now, kind]
            gram = gram_ref[kind]
            for start in range(0, rows, UPDATE_CHUNK):
                cut = slice(start, start + UPDATE_CHUNK)
                own = gram[cut]
                poly = (poly_two * own.astype(jnp.float32) + poly_three * nn(own, gram)).astype(jnp.bfloat16)
                moved = (poly_one * full[cut].astype(jnp.float32) + nn(poly, full)).astype(jnp.bfloat16)
                if sweep < NS_STEPS - 1:
                    x_ref[later, kind, cut] = moved
                else:
                    old = old_ref[kind, cut].astype(jnp.float32)
                    new = old + step_size * moved.astype(jnp.float32)
                    old_mean = jnp.mean(old * old, axis=-1, keepdims=True) + 1e-06
                    new_mean = jnp.mean(new * new, axis=-1, keepdims=True) + 1e-06
                    out_ref[kind, cut] = (new * (jnp.sqrt(old_mean) * lax.rsqrt(new_mean))).astype(jnp.bfloat16)


def masked_rates(rates_ref, seq_ref, split_ref, period):
    rates = rates_ref[...]
    count = rates.shape[1]
    positions = seq_ref[0] * count + lax.broadcasted_iota(jnp.int32, rates.shape, 1)
    early = positions < split_ref[0]
    return jnp.where(early if period == 0 else jnp.logical_not(early), rates, 0.0)


def first_kernel(
    seq_ref,
    split_ref,
    rates_ref,
    weights_hbm,
    keys_hbm,
    values_hbm,
    parts_hbm,
    weights,
    keys,
    values,
    parts,
    sems,
    parts_sems,
):
    copies = {
        "keys": pltpu.make_async_copy(keys_hbm, keys, sems.at[0]),
        "first": pltpu.make_async_copy(weights_hbm.at[0], weights.at[0], sems.at[1]),
        "third": pltpu.make_async_copy(weights_hbm.at[1], weights.at[1], sems.at[2]),
        "values": pltpu.make_async_copy(values_hbm, values, sems.at[3]),
        "second": pltpu.make_async_copy(weights_hbm.at[2], weights.at[2], sems.at[4]),
    }
    for copy in copies.values():
        copy.start()
    rates = masked_rates(rates_ref, seq_ref, split_ref, 0)
    kinds = [weights.at[kind] for kind in range(3)]
    emit_gradient(kinds, keys, values, rates, parts, parts_hbm, parts_sems, lambda name: copies[name].wait())


def second_kernel(
    seq_ref,
    split_ref,
    step_ref,
    rates_ref,
    gathered_hbm,
    weights_hbm,
    keys_hbm,
    values_hbm,
    parts_hbm,
    state_hbm,
    weights,
    keys,
    values,
    x_ref,
    gram_ref,
    state,
    gathered,
    parts,
    sems,
    gathered_sems,
    parts_sems,
):
    fetches = fetch_gathered(gathered_hbm, gathered, gathered_sems)
    fetch_weights = pltpu.make_async_copy(weights_hbm, weights, sems.at[0])
    fetch_keys = pltpu.make_async_copy(keys_hbm, keys, sems.at[1])
    fetch_values = pltpu.make_async_copy(values_hbm, values, sems.at[2])

    def begin():
        fetch_weights.start()
        fetch_keys.start()
        fetch_values.start()

    def load(kind):
        fetches[kind].wait()
        return gathered[kind]

    emit_update(load, weights, step_ref[0], x_ref, gram_ref, state, begin, fetch_weights.wait)
    keep = pltpu.make_async_copy(state, state_hbm, sems.at[3])
    keep.start()
    rates = masked_rates(rates_ref, seq_ref, split_ref, 1)
    fetch_keys.wait()
    fetch_values.wait()
    emit_gradient([state.at[kind] for kind in range(3)], keys, values, rates, parts, parts_hbm, parts_sems)
    keep.wait()


def attend_kernel(
    seq_ref, length_ref, query_ref, keys_ref, values_ref, keys_a_ref, keys_b_ref, values_b_ref, values_c_ref, out_ref
):
    rows, width = query_ref.shape
    branch = seq_ref[0] // BR_SPAN
    place = seq_ref[0] % BR_SPAN
    live = length_ref[branch] - place * rows
    scale = width ** (-0.5)
    prior_keys = jnp.concatenate([keys_a_ref[...], keys_b_ref[...]], axis=0)
    prior_values = jnp.concatenate([values_b_ref[...], values_c_ref[...]], axis=0)
    chunk = 128
    for start in range(0, rows, chunk):
        cut = slice(start, start + chunk)
        query = query_ref[cut]
        row = start + lax.broadcasted_iota(jnp.int32, (chunk, rows), 0)
        slot = lax.broadcasted_iota(jnp.int32, (chunk, rows), 1)
        behind = slot > row
        allowed = (slot == row) | (slot < jnp.where(behind, jnp.where(place > 0, rows, 0), live))
        scores = jnp.where(behind, nt(query, prior_keys), nt(query, keys_ref[...])) * scale
        scores = jnp.where(allowed, scores, -1e30)
        top = jnp.max(scores, axis=-1, keepdims=True)
        power = jnp.exp(scores - top)
        share = power * (1.0 / jnp.sum(power, axis=-1, keepdims=True))
        out_ref[cut] = nn(jnp.where(behind, share, 0.0).astype(jnp.bfloat16), prior_values) + nn(
            jnp.where(behind, 0.0, share).astype(jnp.bfloat16), values_ref[...]
        )


def third_kernel(
    seq_ref,
    split_ref,
    fork_ref,
    step_ref,
    gathered_ref,
    attended_ref,
    weights_hbm,
    state_hbm,
    query_hbm,
    total_ref,
    energy_ref,
    last_hbm,
    old,
    query,
    x_ref,
    gram_ref,
    pool,
    sems,
    trunk_total,
):
    fork = fork_ref[seq_ref[0] // BR_SPAN]
    early = fork < split_ref[0]
    final = jnp.logical_and(jnp.logical_not(early), fork >= trunk_total)
    fetch_old = pltpu.make_async_copy(state_hbm, old, sems.at[0])
    fetch_query = pltpu.make_async_copy(query_hbm, query, sems.at[1])
    fetch_first = pltpu.make_async_copy(weights_hbm, pool.at[1], sems.at[2])
    fetch_state = pltpu.make_async_copy(state_hbm, pool.at[1], sems.at[2])

    def begin():
        fetch_old.start()
        fetch_query.start()

        @pl.when(early)
        def _():
            fetch_first.start()

        @pl.when(jnp.logical_not(early))
        def _():
            fetch_state.start()

    emit_update(lambda kind: gathered_ref[:, kind], old, step_ref[0], x_ref, gram_ref, pool.at[0], begin, fetch_old.wait)
    keep = pltpu.make_async_copy(pool.at[0], last_hbm, sems.at[3])
    keep.start()
    fetch_query.wait()
    fetch_state.wait()
    pick = jnp.where(final, 0, 1)
    rows = query.shape[0]
    for start in range(0, rows, UPDATE_CHUNK):
        cut = slice(start, start + UPDATE_CHUNK)
        first = nt(query[cut], pool[pick, 0])
        third = nt(query[cut], pool[pick, 1])
        hidden = (first * jax.nn.sigmoid(first) * third).astype(jnp.bfloat16)
        total = attended_ref[cut] + nn(hidden, pool[pick, 2])
        total_ref[cut] = total
        energy = jnp.sum(total * total, axis=-1, keepdims=True)
        energy_ref[:, cut] = jnp.transpose(jnp.broadcast_to(energy, (UPDATE_CHUNK, 128)))[0:1]
    keep.wait()


def last_kernel(seq_ref, length_ref, total_ref, energy_ref, gain_ref, out_ref, width):
    rows = total_ref.shape[0]
    live = length_ref[seq_ref[0] // BR_SPAN] - (seq_ref[0] % BR_SPAN) * rows
    slot = lax.broadcasted_iota(jnp.int32, (1, rows), 1)
    inverse = jnp.where(slot < live, lax.rsqrt(energy_ref[...] / width + 1e-06), 0.0)
    columns = jnp.tile(column_of(inverse), (1, total_ref.shape[1] // 128))
    out_ref[...] = (total_ref[...] * columns * gain_ref[...]).astype(jnp.bfloat16)


def replicate_kernel(*refs):
    total = refs[0][...].astype(jnp.float32)
    for ref in refs[1:-1]:
        total = total + ref[...].astype(jnp.float32)
    total = total.astype(jnp.bfloat16)
    for slot in range(refs[-1].shape[0]):
        refs[-1][slot] = total


SMEM = pl.BlockSpec(memory_space=pltpu.SMEM)
VMEM = pl.BlockSpec(memory_space=pltpu.VMEM)
HBM = pl.BlockSpec(memory_space=pltpu.HBM)


def call(kernel, scalars, arrays, outs, held=(), held_outs=(), scratch=(), flops=0, vmem=VMEM_BYTES):
    moved = sum(array.size * array.dtype.itemsize for array in (*arrays, *held, *outs, *held_outs))
    return pl.pallas_call(
        kernel,
        out_shape=(*outs, *held_outs),
        in_specs=[SMEM] * len(scalars) + [VMEM] * len(arrays) + [HBM] * len(held),
        out_specs=[VMEM] * len(outs) + [HBM] * len(held_outs),
        scratch_shapes=list(scratch),
        compiler_params=pltpu.CompilerParams(vmem_limit_bytes=vmem),
        cost_estimate=pl.CostEstimate(flops=flops, bytes_accessed=moved, transcendentals=0),
    )(*scalars, *arrays, *held)


def shape(dims, kind):
    return jax.ShapeDtypeStruct(dims, kind)


def space(dims, kind=jnp.bfloat16):
    return pltpu.VMEM(dims, kind)


def gradient_first(seq, split, rates, weights, keys, values, parts_shape):
    scratch = (
        space(weights.shape),
        space(keys.shape),
        space(values.shape),
        space(parts_shape.shape),
        pltpu.SemaphoreType.DMA((5,)),
        pltpu.SemaphoreType.DMA((3 * keys.shape[0] // CHUNK,)),
    )
    (parts,) = call(
        first_kernel,
        (seq, split),
        (rates,),
        (),
        (weights, keys, values),
        (parts_shape,),
        scratch,
        flops=12 * keys.size * weights.shape[1],
        vmem=WHOLE_VMEM,
    )
    return parts


def by_kind(gathered):
    planes, kinds, step, width = gathered.shape
    return space((kinds, planes, step, width))


def update_and_gradient(seq, split, step, gathered, rates, weights, keys, values):
    full = weights.shape
    scratch = (
        space(full),
        space(keys.shape),
        space(values.shape),
        space((2, *full)),
        space(full),
        space(full),
        by_kind(gathered),
        space(gathered.shape),
        pltpu.SemaphoreType.DMA((4,)),
        pltpu.SemaphoreType.DMA((3,)),
        pltpu.SemaphoreType.DMA((3 * full[1] // CHUNK,)),
    )
    return call(
        second_kernel,
        (seq, split, step),
        (rates,),
        (),
        (gathered, weights, keys, values),
        (shape(gathered.shape, jnp.bfloat16), shape(full, jnp.bfloat16)),
        scratch,
        flops=48 * keys.size * full[1],
        vmem=SECOND_VMEM,
    )


def update_and_apply(seq, split, forks, step, gathered, weights, state, query, attended, trunk_total):
    full = weights.shape
    rows, width = query.shape
    scratch = (
        space(full),
        space(query.shape),
        space((2, *full)),
        space(full),
        space((2, *full)),
        pltpu.SemaphoreType.DMA((4,)),
    )
    return call(
        functools.partial(third_kernel, trunk_total=trunk_total),
        (seq, split, forks, step),
        (gathered, attended),
        (shape((rows, width), jnp.float32), shape((1, rows), jnp.float32)),
        (weights, state, query),
        (shape(full, jnp.bfloat16),),
        scratch,
        flops=42 * query.size * full[1],
        vmem=LAST_VMEM,
    )


def from_behind(value):
    count = lax.axis_size("z")
    return lax.ppermute(value, "z", [(source, source + 1) for source in range(count - 1)])


def sum_plane(parts):
    received = lax.all_to_all(parts, PLANE, 0, 0, tiled=False)
    return jnp.sum(received.astype(jnp.float32), axis=0).astype(jnp.bfloat16)


def swap_depth(value, flip):
    depth = lax.axis_size("z")
    return lax.ppermute(value, "z", [(i, i ^ flip) for i in range(depth)])


def sum_depth(mine, beside=None):
    planes = lax.axis_size(PLANE)
    other, beside = lax.optimization_barrier((swap_depth(mine, 1), beside))
    pair = (mine.astype(jnp.float32) + other.astype(jnp.float32)).astype(jnp.bfloat16)
    (copies,) = call(
        replicate_kernel, (), (pair, swap_depth(pair, 3)), (shape((planes, *mine.shape), mine.dtype),)
    )
    return copies, beside


def spread_plane(copies):
    return lax.all_to_all(copies, PLANE, 0, 0, tiled=False)


def per_device(
    trunk_keys,
    trunk_values,
    trunk_rates,
    segment_end,
    fast_weights,
    step_sizes,
    branch_query,
    branch_keys,
    branch_values,
    branch_lengths,
    fork_points,
    out_gain,
):
    keys, values = trunk_keys[0], trunk_values[0]
    weights = fast_weights[:, 0]
    query, own_keys, own_values = branch_query[0], branch_keys[0], branch_values[0]
    rows, width = keys.shape
    hidden = weights.shape[1]
    planes = lax.axis_size(PLANE)
    trunk_total = rows * lax.axis_size(SEQ)
    total_width = width * lax.axis_size(HEAD)
    seq = lax.axis_index(SEQ).astype(jnp.int32).reshape(1)
    parts_shape = shape((planes, 3, hidden // planes, width), jnp.bfloat16)
    barrier = lax.optimization_barrier
    most = 3 * rows // 4

    keys_a = from_behind(own_keys[:most])
    parts = gradient_first(seq, segment_end, trunk_rates, weights, keys, values, parts_shape)
    mine, keys_a = barrier((sum_plane(parts), keys_a))
    copies, _ = sum_depth(mine)
    copies, rest_keys, rest_values = barrier((copies, own_keys[most:], own_values[: rows - most]))
    gathered, keys_b, values_b = barrier((spread_plane(copies), from_behind(rest_keys), from_behind(rest_values)))
    parts, state = update_and_gradient(
        seq, segment_end, step_sizes, gathered, trunk_rates, weights, keys, values
    )
    parts, rest_values = barrier((parts, own_values[rows - most :]))
    mine, values_c, query = barrier((sum_plane(parts), from_behind(rest_values), query))
    (attended,) = call(
        attend_kernel,
        (seq, branch_lengths),
        (query, own_keys, own_values, keys_a, keys_b, values_b, values_c),
        (shape((rows, width), jnp.float32),),
        flops=8 * rows * rows * width,
    )
    copies, attended = sum_depth(mine, attended)
    gathered = spread_plane(copies)
    total, energy, last = update_and_apply(
        seq, segment_end, fork_points, step_sizes, gathered, weights, state, query, attended, trunk_total
    )
    energy = lax.psum(energy, HEAD)
    (result,) = call(
        functools.partial(last_kernel, width=total_width),
        (seq, branch_lengths),
        (total, energy, out_gain),
        (shape((rows, width), jnp.bfloat16),),
    )
    return (result[None], last[:, None])


def solution(mesh):
    fine = Mesh(mesh.devices.reshape(4, 4, 4, 2, 2), (*SEQ, *HEAD))
    rows = P(HEAD, SEQ, None)
    placed = (
        rows,
        rows,
        P(HEAD, SEQ),
        P(),
        P(None, HEAD, None, None),
        P(HEAD),
        rows,
        rows,
        rows,
        P(),
        P(),
        P(HEAD, None),
    )
    return jax.shard_map(
        per_device,
        mesh=fine,
        in_specs=placed,
        out_specs=(rows, P(None, HEAD, None, None)),
        check_vma=False,
    )
```

```python
import functools
import jax
import jax.numpy as jnp
from jax import lax
from jax.experimental import pallas as pl
from jax.experimental.pallas import tpu as pltpu
from jax.sharding import Mesh
from jax.sharding import PartitionSpec as P

PLANE = ("x", "y")
SEQ = ("x", "y", "z")
HEAD = ("w", "c")
NS_STEPS = 2
BR_SPAN = 4

poly_one = 3.4445
poly_two = -4.775
poly_three = 2.0315
VMEM_BYTES = 24 * 1024 * 1024
WHOLE_VMEM = 60 * 1024 * 1024
LAST_VMEM = 46 * 1024 * 1024
SECOND_VMEM = 60 * 1024 * 1024
CHUNK = 256
UPDATE_CHUNK = 512


def nt(left, right):
    return lax.dot_general(left, right, (((1,), (1,)), ((), ())), preferred_element_type=jnp.float32)


def nn(left, right):
    return jnp.dot(left, right, preferred_element_type=jnp.float32)


def column_of(row):
    return jnp.transpose(jnp.broadcast_to(row, (128, row.shape[1])))


def emit_gradient(weights, keys_ref, values_ref, rates, parts_ref, parts_hbm, sems, ready=lambda name: None):
    step = parts_ref.shape[2]
    sent = []
    rows, width = weights[0].shape
    ready("keys")
    keys = keys_ref[...]
    pushed = None
    for start in range(0, rows, CHUNK):
        cut = slice(start, start + CHUNK)
        if start == 0:
            ready("first")
        first = nt(weights[0][cut], keys)
        if start == 0:
            ready("third")
        third = nt(weights[1][cut], keys)
        gate = jax.nn.sigmoid(first)
        silu = first * gate
        hidden = (silu * third).astype(jnp.bfloat16)
        if start == 0:
            ready("rates")
            rate_columns = jnp.tile(column_of(rates()), (1, width // 128))
            ready("values")
            pushed = (rate_columns * values_ref[...].astype(jnp.float32)).astype(jnp.bfloat16)
            ready("second")
        returned = nt(weights[2][cut], pushed)
        delta_first = (returned * third * gate * (1.0 + first * (1.0 - gate))).astype(jnp.bfloat16)
        delta_third = (returned * silu).astype(jnp.bfloat16)
        for kind, grad in enumerate((nn(delta_first, keys), nn(delta_third, keys), nn(hidden, pushed))):
            grad = grad.astype(jnp.bfloat16)
            for part in range(CHUNK // step):
                parts_ref[start // step + part, kind] = grad[part * step : (part + 1) * step]
            slots = pl.ds(start // step, CHUNK // step)
            copy = pltpu.make_async_copy(
                parts_ref.at[slots, kind], parts_hbm.at[slots, kind], sems.at[len(sent)]
            )
            copy.start()
            sent.append(copy)
    for copy in sent:
        copy.wait()


def fetch_gathered(gathered_hbm, gathered_ref, sems):
    copies = [
        pltpu.make_async_copy(gathered_hbm.at[:, kind], gathered_ref.at[kind], sems.at[kind])
        for kind in range(gathered_ref.shape[0])
    ]
    for copy in copies:
        copy.start()
    return copies


def emit_update(load, old_ref, step_size, x_ref, gram_ref, out_ref, begin, ready):
    kinds, rows, width = out_ref.shape
    for kind in range(kinds):
        wide = load(kind).reshape(rows, width).astype(jnp.float32)
        square = jnp.sum(jnp.sum(wide * wide, axis=0, keepdims=True), axis=1, keepdims=True)
        inverse = 1.0 / (jnp.sqrt(square) + 1e-07)
        x_ref[0, kind] = (wide * inverse).astype(jnp.bfloat16)
    begin()
    for sweep in range(NS_STEPS):
        now, later = sweep % 2, (sweep + 1) % 2
        if sweep == NS_STEPS - 1:
            ready()
        for kind in range(kinds):
            full = x_ref[now, kind]
            gram_ref[kind] = nt(full, full).astype(jnp.bfloat16)
        for kind in range(kinds):
            full = x_ref[now, kind]
            gram = gram_ref[kind]
            for start in range(0, rows, UPDATE_CHUNK):
                cut = slice(start, start + UPDATE_CHUNK)
                own = gram[cut]
                poly = (poly_two * own.astype(jnp.float32) + poly_three * nn(own, gram)).astype(jnp.bfloat16)
                moved = (poly_one * full[cut].astype(jnp.float32) + nn(poly, full)).astype(jnp.bfloat16)
                if sweep < NS_STEPS - 1:
                    x_ref[later, kind, cut] = moved
                else:
                    old = old_ref[kind, cut].astype(jnp.float32)
                    new = old + step_size * moved.astype(jnp.float32)
                    old_mean = jnp.mean(old * old, axis=-1, keepdims=True) + 1e-06
                    new_mean = jnp.mean(new * new, axis=-1, keepdims=True) + 1e-06
                    out_ref[kind, cut] = (new * (jnp.sqrt(old_mean) * lax.rsqrt(new_mean))).astype(jnp.bfloat16)


def place_in_seq():
    return lax.axis_index(SEQ).astype(jnp.int32)


def masked_rates(rates, split_ref, period):
    count = rates.shape[1]
    positions = place_in_seq() * count + lax.broadcasted_iota(jnp.int32, rates.shape, 1)
    early = positions < split_ref[0]
    return jnp.where(early if period == 0 else jnp.logical_not(early), rates, 0.0)


def first_kernel(
    split_ref,
    rates_hbm,
    weights_hbm,
    keys_hbm,
    values_hbm,
    parts_hbm,
    rates,
    weights,
    keys,
    values,
    parts,
    sems,
    parts_sems,
):
    copies = {
        "keys": pltpu.make_async_copy(keys_hbm, keys, sems.at[0]),
        "first": pltpu.make_async_copy(weights_hbm.at[0], weights.at[0], sems.at[1]),
        "third": pltpu.make_async_copy(weights_hbm.at[1], weights.at[1], sems.at[2]),
        "values": pltpu.make_async_copy(values_hbm, values, sems.at[3]),
        "second": pltpu.make_async_copy(weights_hbm.at[2], weights.at[2], sems.at[4]),
        "rates": pltpu.make_async_copy(rates_hbm, rates, sems.at[5]),
    }
    for copy in copies.values():
        copy.start()
    kinds = [weights.at[kind] for kind in range(3)]
    emit_gradient(kinds, keys, values, lambda: masked_rates(rates[...], split_ref, 0), parts, parts_hbm, parts_sems, lambda name: copies[name].wait())


def second_kernel(
    split_ref,
    step_ref,
    rates_hbm,
    gathered_hbm,
    weights_hbm,
    keys_hbm,
    values_hbm,
    parts_hbm,
    state_hbm,
    rates,
    weights,
    keys,
    values,
    x_ref,
    gram_ref,
    state,
    gathered,
    parts,
    sems,
    gathered_sems,
    parts_sems,
):
    fetches = fetch_gathered(gathered_hbm, gathered, gathered_sems)
    fetch_weights = pltpu.make_async_copy(weights_hbm, weights, sems.at[0])
    fetch_keys = pltpu.make_async_copy(keys_hbm, keys, sems.at[1])
    fetch_values = pltpu.make_async_copy(values_hbm, values, sems.at[2])
    fetch_rates = pltpu.make_async_copy(rates_hbm, rates, sems.at[4])

    def begin():
        fetch_weights.start()
        fetch_keys.start()
        fetch_values.start()
        fetch_rates.start()

    def load(kind):
        fetches[kind].wait()
        return gathered[kind]

    emit_update(load, weights, step_ref[0], x_ref, gram_ref, state, begin, fetch_weights.wait)
    keep = pltpu.make_async_copy(state, state_hbm, sems.at[3])
    keep.start()
    fetch_keys.wait()
    fetch_values.wait()
    fetch_rates.wait()
    kinds = [state.at[kind] for kind in range(3)]
    emit_gradient(kinds, keys, values, lambda: masked_rates(rates[...], split_ref, 1), parts, parts_hbm, parts_sems)
    keep.wait()


def attend_kernel(
    length_ref, query_ref, keys_ref, values_ref, keys_a_ref, both_b_ref, values_c_ref, out_ref
):
    rows, width = query_ref.shape
    seq = place_in_seq()
    branch = seq // BR_SPAN
    place = seq % BR_SPAN
    live = length_ref[branch] - place * rows
    scale = width ** (-0.5)
    rest = rows - keys_a_ref.shape[0]
    prior_keys = jnp.concatenate([keys_a_ref[...], both_b_ref[:rest]], axis=0)
    prior_values = jnp.concatenate([both_b_ref[rest:], values_c_ref[...]], axis=0)
    chunk = 128
    for start in range(0, rows, chunk):
        cut = slice(start, start + chunk)
        query = query_ref[cut]
        row = start + lax.broadcasted_iota(jnp.int32, (chunk, rows), 0)
        slot = lax.broadcasted_iota(jnp.int32, (chunk, rows), 1)
        behind = slot > row
        allowed = (slot == row) | (slot < jnp.where(behind, jnp.where(place > 0, rows, 0), live))
        scores = jnp.where(behind, nt(query, prior_keys), nt(query, keys_ref[...])) * scale
        scores = jnp.where(allowed, scores, -1e30)
        top = jnp.max(scores, axis=-1, keepdims=True)
        power = jnp.exp(scores - top)
        share = power * (1.0 / jnp.sum(power, axis=-1, keepdims=True))
        out_ref[cut] = nn(jnp.where(behind, share, 0.0).astype(jnp.bfloat16), prior_values) + nn(
            jnp.where(behind, 0.0, share).astype(jnp.bfloat16), values_ref[...]
        )


def third_kernel(
    split_ref,
    fork_ref,
    step_ref,
    gathered_ref,
    attended_ref,
    weights_hbm,
    state_hbm,
    query_hbm,
    total_ref,
    energy_ref,
    last_hbm,
    old,
    query,
    x_ref,
    gram_ref,
    pool,
    sems,
    trunk_total,
):
    fork = fork_ref[place_in_seq() // BR_SPAN]
    early = fork < split_ref[0]
    final = jnp.logical_and(jnp.logical_not(early), fork >= trunk_total)
    fetch_old = pltpu.make_async_copy(state_hbm, old, sems.at[0])
    fetch_query = pltpu.make_async_copy(query_hbm, query, sems.at[1])
    fetch_first = pltpu.make_async_copy(weights_hbm, pool.at[1], sems.at[2])
    fetch_state = pltpu.make_async_copy(state_hbm, pool.at[1], sems.at[2])

    def begin():
        fetch_old.start()
        fetch_query.start()

        @pl.when(early)
        def _():
            fetch_first.start()

        @pl.when(jnp.logical_not(early))
        def _():
            fetch_state.start()

    emit_update(lambda kind: gathered_ref[:, kind], old, step_ref[0], x_ref, gram_ref, pool.at[0], begin, fetch_old.wait)
    keep = pltpu.make_async_copy(pool.at[0], last_hbm, sems.at[3])
    keep.start()
    fetch_query.wait()
    fetch_state.wait()
    pick = jnp.where(final, 0, 1)
    rows = query.shape[0]
    for start in range(0, rows, UPDATE_CHUNK):
        cut = slice(start, start + UPDATE_CHUNK)
        first = nt(query[cut], pool[pick, 0])
        third = nt(query[cut], pool[pick, 1])
        hidden = (first * jax.nn.sigmoid(first) * third).astype(jnp.bfloat16)
        total = attended_ref[cut] + nn(hidden, pool[pick, 2])
        total_ref[cut] = total
        energy = jnp.sum(total * total, axis=-1, keepdims=True)
        energy_ref[:, cut] = jnp.transpose(jnp.broadcast_to(energy, (UPDATE_CHUNK, 128)))[0:1]
    keep.wait()


def last_kernel(length_ref, total_ref, energy_ref, gain_ref, out_ref, width):
    rows = total_ref.shape[0]
    seq = place_in_seq()
    live = length_ref[seq // BR_SPAN] - (seq % BR_SPAN) * rows
    slot = lax.broadcasted_iota(jnp.int32, (1, rows), 1)
    inverse = jnp.where(slot < live, lax.rsqrt(energy_ref[...] / width + 1e-06), 0.0)
    columns = jnp.tile(column_of(inverse), (1, total_ref.shape[1] // 128))
    out_ref[...] = (total_ref[...] * columns * gain_ref[...]).astype(jnp.bfloat16)


def replicate_kernel(*refs):
    total = refs[0][...].astype(jnp.float32)
    for ref in refs[1:-1]:
        total = total + ref[...].astype(jnp.float32)
    total = total.astype(jnp.bfloat16)
    for slot in range(refs[-1].shape[0]):
        refs[-1][slot] = total


SMEM = pl.BlockSpec(memory_space=pltpu.SMEM)
VMEM = pl.BlockSpec(memory_space=pltpu.VMEM)
HBM = pl.BlockSpec(memory_space=pltpu.HBM)


def call(kernel, scalars, arrays, outs, held=(), held_outs=(), scratch=(), flops=0, vmem=VMEM_BYTES):
    moved = sum(array.size * array.dtype.itemsize for array in (*arrays, *held, *outs, *held_outs))
    return pl.pallas_call(
        kernel,
        out_shape=(*outs, *held_outs),
        in_specs=[SMEM] * len(scalars) + [VMEM] * len(arrays) + [HBM] * len(held),
        out_specs=[VMEM] * len(outs) + [HBM] * len(held_outs),
        scratch_shapes=list(scratch),
        compiler_params=pltpu.CompilerParams(vmem_limit_bytes=vmem),
        cost_estimate=pl.CostEstimate(flops=flops, bytes_accessed=moved, transcendentals=0),
    )(*scalars, *arrays, *held)


def shape(dims, kind):
    return jax.ShapeDtypeStruct(dims, kind)


def space(dims, kind=jnp.bfloat16):
    return pltpu.VMEM(dims, kind)


def gradient_first(split, rates, weights, keys, values, parts_shape):
    scratch = (
        space(rates.shape, rates.dtype),
        space(weights.shape),
        space(keys.shape),
        space(values.shape),
        space(parts_shape.shape),
        pltpu.SemaphoreType.DMA((6,)),
        pltpu.SemaphoreType.DMA((3 * keys.shape[0] // CHUNK,)),
    )
    (parts,) = call(
        first_kernel,
        (split,),
        (),
        (),
        (rates, weights, keys, values),
        (parts_shape,),
        scratch,
        flops=12 * keys.size * weights.shape[1],
        vmem=WHOLE_VMEM,
    )
    return parts


def by_kind(gathered):
    planes, kinds, step, width = gathered.shape
    return space((kinds, planes, step, width))


def update_and_gradient(split, step, gathered, rates, weights, keys, values):
    full = weights.shape
    scratch = (
        space(rates.shape, rates.dtype),
        space(full),
        space(keys.shape),
        space(values.shape),
        space((2, *full)),
        space(full),
        space(full),
        by_kind(gathered),
        space(gathered.shape),
        pltpu.SemaphoreType.DMA((5,)),
        pltpu.SemaphoreType.DMA((3,)),
        pltpu.SemaphoreType.DMA((3 * full[1] // CHUNK,)),
    )
    return call(
        second_kernel,
        (split, step),
        (),
        (),
        (rates, gathered, weights, keys, values),
        (shape(gathered.shape, jnp.bfloat16), shape(full, jnp.bfloat16)),
        scratch,
        flops=48 * keys.size * full[1],
        vmem=SECOND_VMEM,
    )


def update_and_apply(split, forks, step, gathered, weights, state, query, attended, trunk_total):
    full = weights.shape
    rows, width = query.shape
    scratch = (
        space(full),
        space(query.shape),
        space((2, *full)),
        space(full),
        space((2, *full)),
        pltpu.SemaphoreType.DMA((4,)),
    )
    return call(
        functools.partial(third_kernel, trunk_total=trunk_total),
        (split, forks, step),
        (gathered, attended),
        (shape((rows, width), jnp.float32), shape((1, rows), jnp.float32)),
        (weights, state, query),
        (shape(full, jnp.bfloat16),),
        scratch,
        flops=42 * query.size * full[1],
        vmem=LAST_VMEM,
    )


def from_behind(value):
    count = lax.axis_size("z")
    return lax.ppermute(value, "z", [(source, source + 1) for source in range(count - 1)])


def sum_plane(parts):
    received = lax.all_to_all(parts, PLANE, 0, 0, tiled=False)
    return jnp.sum(received.astype(jnp.float32), axis=0).astype(jnp.bfloat16)


def swap_depth(value, flip):
    depth = lax.axis_size("z")
    return lax.ppermute(value, "z", [(i, i ^ flip) for i in range(depth)])


def sum_depth(mine, beside=None):
    planes = lax.axis_size(PLANE)
    other, beside = lax.optimization_barrier((swap_depth(mine, 1), beside))
    pair = (mine.astype(jnp.float32) + other.astype(jnp.float32)).astype(jnp.bfloat16)
    (copies,) = call(
        replicate_kernel, (), (pair, swap_depth(pair, 3)), (shape((planes, *mine.shape), mine.dtype),)
    )
    return copies, beside


def spread_plane(copies):
    return lax.all_to_all(copies, PLANE, 0, 0, tiled=False)


def per_device(
    trunk_keys,
    trunk_values,
    trunk_rates,
    segment_end,
    fast_weights,
    step_sizes,
    branch_query,
    branch_keys,
    branch_values,
    branch_lengths,
    fork_points,
    out_gain,
):
    keys, values = trunk_keys[0], trunk_values[0]
    weights = fast_weights[:, 0]
    query, own_keys, own_values = branch_query[0], branch_keys[0], branch_values[0]
    rows, width = keys.shape
    hidden = weights.shape[1]
    planes = lax.axis_size(PLANE)
    trunk_total = rows * lax.axis_size(SEQ)
    total_width = width * lax.axis_size(HEAD)
    parts_shape = shape((planes, 3, hidden // planes, width), jnp.bfloat16)
    barrier = lax.optimization_barrier
    most = 3 * rows // 4

    keys_a = from_behind(own_keys[:most])
    parts = gradient_first(segment_end, trunk_rates, weights, keys, values, parts_shape)
    mine, keys_a = barrier((sum_plane(parts), keys_a))
    copies, _ = sum_depth(mine)
    copies, rest = barrier((copies, jnp.concatenate([own_keys[most:], own_values[: rows - most]], axis=0)))
    gathered, both_b = barrier((spread_plane(copies), from_behind(rest)))
    parts, state = update_and_gradient(
        segment_end, step_sizes, gathered, trunk_rates, weights, keys, values
    )
    parts, rest_values = barrier((parts, own_values[rows - most :]))
    mine, values_c, query = barrier((sum_plane(parts), from_behind(rest_values), query))
    (attended,) = call(
        attend_kernel,
        (branch_lengths,),
        (query, own_keys, own_values, keys_a, both_b, values_c),
        (shape((rows, width), jnp.float32),),
        flops=8 * rows * rows * width,
    )
    copies, attended = sum_depth(mine, attended)
    gathered = spread_plane(copies)
    total, energy, last = update_and_apply(
        segment_end, fork_points, step_sizes, gathered, weights, state, query, attended, trunk_total
    )
    energy = lax.psum(energy, HEAD)
    (result,) = call(
        functools.partial(last_kernel, width=total_width),
        (branch_lengths,),
        (total, energy, out_gain),
        (shape((rows, width), jnp.bfloat16),),
    )
    return (result[None], last[:, None])


def solution(mesh):
    fine = Mesh(mesh.devices.reshape(4, 4, 4, 2, 2), (*SEQ, *HEAD))
    rows = P(HEAD, SEQ, None)
    placed = (
        rows,
        rows,
        P(HEAD, SEQ),
        P(),
        P(None, HEAD, None, None),
        P(HEAD),
        rows,
        rows,
        rows,
        P(),
        P(),
        P(HEAD, None),
    )
    return jax.shard_map(
        per_device,
        mesh=fine,
        in_specs=placed,
        out_specs=(rows, P(None, HEAD, None, None)),
        check_vma=False,
    )
```

```python
import functools
import jax
import jax.numpy as jnp
from jax import lax
from jax.experimental import pallas as pl
from jax.experimental.pallas import tpu as pltpu
from jax.sharding import Mesh
from jax.sharding import PartitionSpec as P

PLANE = ("x", "y")
SEQ = ("x", "y", "z")
HEAD = ("w", "c")
NS_STEPS = 2
BR_SPAN = 4

poly_one = 3.4445
poly_two = -4.775
poly_three = 2.0315
VMEM_BYTES = 24 * 1024 * 1024
WHOLE_VMEM = 60 * 1024 * 1024
LAST_VMEM = 46 * 1024 * 1024
SECOND_VMEM = 61 * 1024 * 1024
CHUNK = 256
UPDATE_CHUNK = 512


def nt(left, right):
    return lax.dot_general(left, right, (((1,), (1,)), ((), ())), preferred_element_type=jnp.float32)


def nn(left, right):
    return jnp.dot(left, right, preferred_element_type=jnp.float32)


def column_of(row):
    return jnp.transpose(jnp.broadcast_to(row, (128, row.shape[1])))


def emit_gradient(weights, keys_ref, values_ref, rates, parts_ref, parts_hbm, sems, ready=lambda name: None):
    step = parts_ref.shape[2]
    sent = []
    rows, width = weights[0].shape
    ready("keys")
    keys = keys_ref[...]
    pushed = None
    for start in range(0, rows, CHUNK):
        cut = slice(start, start + CHUNK)
        if start == 0:
            ready("first")
        first = nt(weights[0][cut], keys)
        if start == 0:
            ready("third")
        third = nt(weights[1][cut], keys)
        gate = jax.nn.sigmoid(first)
        silu = first * gate
        hidden = (silu * third).astype(jnp.bfloat16)
        if start == 0:
            ready("rates")
            rate_columns = jnp.tile(column_of(rates()), (1, width // 128))
            ready("values")
            pushed = (rate_columns * values_ref[...].astype(jnp.float32)).astype(jnp.bfloat16)
            ready("second")
        returned = nt(weights[2][cut], pushed)
        delta_first = (returned * third * gate * (1.0 + first * (1.0 - gate))).astype(jnp.bfloat16)
        delta_third = (returned * silu).astype(jnp.bfloat16)
        for kind, grad in enumerate((nn(delta_first, keys), nn(delta_third, keys), nn(hidden, pushed))):
            grad = grad.astype(jnp.bfloat16)
            for part in range(CHUNK // step):
                parts_ref[start // step + part, kind] = grad[part * step : (part + 1) * step]
            slots = pl.ds(start // step, CHUNK // step)
            copy = pltpu.make_async_copy(
                parts_ref.at[slots, kind], parts_hbm.at[slots, kind], sems.at[len(sent)]
            )
            copy.start()
            sent.append(copy)
    for copy in sent:
        copy.wait()


def fetch_gathered(gathered_hbm, gathered_ref, sems):
    copies = [
        pltpu.make_async_copy(gathered_hbm.at[:, kind], gathered_ref.at[kind], sems.at[kind])
        for kind in range(gathered_ref.shape[0])
    ]
    for copy in copies:
        copy.start()
    return copies


def emit_update(load, old_ref, step_size, x_ref, gram_ref, out_ref, begin, ready):
    kinds, rows, width = out_ref.shape
    for kind in range(kinds):
        wide = load(kind).reshape(rows, width).astype(jnp.float32)
        square = jnp.sum(jnp.sum(wide * wide, axis=0, keepdims=True), axis=1, keepdims=True)
        inverse = 1.0 / (jnp.sqrt(square) + 1e-07)
        x_ref[0, kind] = (wide * inverse).astype(jnp.bfloat16)
    begin()
    for sweep in range(NS_STEPS):
        now, later = sweep % 2, (sweep + 1) % 2
        if sweep == NS_STEPS - 1:
            ready()
        for kind in range(kinds):
            full = x_ref[now, kind]
            gram_ref[kind] = nt(full, full).astype(jnp.bfloat16)
        for kind in range(kinds):
            full = x_ref[now, kind]
            gram = gram_ref[kind]
            for start in range(0, rows, UPDATE_CHUNK):
                cut = slice(start, start + UPDATE_CHUNK)
                own = gram[cut]
                poly = (poly_two * own.astype(jnp.float32) + poly_three * nn(own, gram)).astype(jnp.bfloat16)
                moved = (poly_one * full[cut].astype(jnp.float32) + nn(poly, full)).astype(jnp.bfloat16)
                if sweep < NS_STEPS - 1:
                    x_ref[later, kind, cut] = moved
                else:
                    old = old_ref[kind, cut].astype(jnp.float32)
                    new = old + step_size * moved.astype(jnp.float32)
                    old_mean = jnp.mean(old * old, axis=-1, keepdims=True) + 1e-06
                    new_mean = jnp.mean(new * new, axis=-1, keepdims=True) + 1e-06
                    out_ref[kind, cut] = (new * (jnp.sqrt(old_mean) * lax.rsqrt(new_mean))).astype(jnp.bfloat16)


def place_in_seq():
    return lax.axis_index(SEQ).astype(jnp.int32)


def masked_rates(rates, split_ref, period):
    count = rates.shape[1]
    positions = place_in_seq() * count + lax.broadcasted_iota(jnp.int32, rates.shape, 1)
    early = positions < split_ref[0]
    return jnp.where(early if period == 0 else jnp.logical_not(early), rates, 0.0)


def first_kernel(
    split_ref,
    rates_hbm,
    weights_hbm,
    keys_hbm,
    values_hbm,
    parts_hbm,
    rates,
    weights,
    keys,
    values,
    parts,
    sems,
    parts_sems,
):
    copies = {
        "keys": pltpu.make_async_copy(keys_hbm, keys, sems.at[0]),
        "first": pltpu.make_async_copy(weights_hbm.at[0], weights.at[0], sems.at[1]),
        "third": pltpu.make_async_copy(weights_hbm.at[1], weights.at[1], sems.at[2]),
        "values": pltpu.make_async_copy(values_hbm, values, sems.at[3]),
        "second": pltpu.make_async_copy(weights_hbm.at[2], weights.at[2], sems.at[4]),
        "rates": pltpu.make_async_copy(rates_hbm, rates, sems.at[5]),
    }
    for copy in copies.values():
        copy.start()
    kinds = [weights.at[kind] for kind in range(3)]
    emit_gradient(kinds, keys, values, lambda: masked_rates(rates[...], split_ref, 0), parts, parts_hbm, parts_sems, lambda name: copies[name].wait())


def second_kernel(
    split_ref,
    step_ref,
    rates_hbm,
    gathered_hbm,
    weights_hbm,
    keys_hbm,
    values_hbm,
    parts_hbm,
    state_hbm,
    rates,
    weights,
    keys,
    values,
    x_ref,
    gram_ref,
    state,
    gathered,
    parts,
    sems,
    gathered_sems,
    parts_sems,
):
    fetches = fetch_gathered(gathered_hbm, gathered, gathered_sems)
    fetch_weights = pltpu.make_async_copy(weights_hbm, weights, sems.at[0])
    fetch_keys = pltpu.make_async_copy(keys_hbm, keys, sems.at[1])
    fetch_values = pltpu.make_async_copy(values_hbm, values, sems.at[2])
    fetch_rates = pltpu.make_async_copy(rates_hbm, rates, sems.at[4])

    def begin():
        fetch_weights.start()
        fetch_keys.start()
        fetch_values.start()
        fetch_rates.start()

    def load(kind):
        fetches[kind].wait()
        return gathered[kind]

    emit_update(load, weights, step_ref[0], x_ref, gram_ref, state, begin, fetch_weights.wait)
    keep = pltpu.make_async_copy(state, state_hbm, sems.at[3])
    keep.start()
    fetch_keys.wait()
    fetch_values.wait()
    fetch_rates.wait()
    kinds = [state.at[kind] for kind in range(3)]
    emit_gradient(kinds, keys, values, lambda: masked_rates(rates[...], split_ref, 1), parts, parts_hbm, parts_sems)
    keep.wait()


def attend_kernel(
    length_ref, query_ref, keys_ref, values_ref, keys_a_ref, keys_b_ref, values_b_ref, values_c_ref, out_ref
):
    rows, width = query_ref.shape
    seq = place_in_seq()
    branch = seq // BR_SPAN
    place = seq % BR_SPAN
    live = length_ref[branch] - place * rows
    scale = width ** (-0.5)
    prior_keys = jnp.concatenate([keys_a_ref[...], keys_b_ref[...]], axis=0)
    prior_values = jnp.concatenate([values_b_ref[...], values_c_ref[...]], axis=0)
    chunk = 128
    for start in range(0, rows, chunk):
        cut = slice(start, start + chunk)
        query = query_ref[cut]
        row = start + lax.broadcasted_iota(jnp.int32, (chunk, rows), 0)
        slot = lax.broadcasted_iota(jnp.int32, (chunk, rows), 1)
        behind = slot > row
        allowed = (slot == row) | (slot < jnp.where(behind, jnp.where(place > 0, rows, 0), live))
        scores = jnp.where(behind, nt(query, prior_keys), nt(query, keys_ref[...])) * scale
        scores = jnp.where(allowed, scores, -1e30)
        top = jnp.max(scores, axis=-1, keepdims=True)
        power = jnp.exp(scores - top)
        share = power * (1.0 / jnp.sum(power, axis=-1, keepdims=True))
        out_ref[cut] = nn(jnp.where(behind, share, 0.0).astype(jnp.bfloat16), prior_values) + nn(
            jnp.where(behind, 0.0, share).astype(jnp.bfloat16), values_ref[...]
        )


def third_kernel(
    split_ref,
    fork_ref,
    step_ref,
    gathered_ref,
    attended_ref,
    weights_hbm,
    state_hbm,
    query_hbm,
    total_ref,
    energy_ref,
    last_hbm,
    old,
    query,
    x_ref,
    gram_ref,
    pool,
    sems,
    trunk_total,
):
    fork = fork_ref[place_in_seq() // BR_SPAN]
    early = fork < split_ref[0]
    final = jnp.logical_and(jnp.logical_not(early), fork >= trunk_total)
    fetch_old = pltpu.make_async_copy(state_hbm, old, sems.at[0])
    fetch_query = pltpu.make_async_copy(query_hbm, query, sems.at[1])
    fetch_first = pltpu.make_async_copy(weights_hbm, pool.at[1], sems.at[2])
    fetch_state = pltpu.make_async_copy(state_hbm, pool.at[1], sems.at[2])

    def begin():
        fetch_old.start()
        fetch_query.start()

        @pl.when(early)
        def _():
            fetch_first.start()

        @pl.when(jnp.logical_not(early))
        def _():
            fetch_state.start()

    emit_update(lambda kind: gathered_ref[:, kind], old, step_ref[0], x_ref, gram_ref, pool.at[0], begin, fetch_old.wait)
    keep = pltpu.make_async_copy(pool.at[0], last_hbm, sems.at[3])
    keep.start()
    fetch_query.wait()
    fetch_state.wait()
    pick = jnp.where(final, 0, 1)
    rows = query.shape[0]
    for start in range(0, rows, UPDATE_CHUNK):
        cut = slice(start, start + UPDATE_CHUNK)
        first = nt(query[cut], pool[pick, 0])
        third = nt(query[cut], pool[pick, 1])
        hidden = (first * jax.nn.sigmoid(first) * third).astype(jnp.bfloat16)
        total = attended_ref[cut] + nn(hidden, pool[pick, 2])
        total_ref[cut] = total
        energy = jnp.sum(total * total, axis=-1, keepdims=True)
        energy_ref[:, cut] = jnp.transpose(jnp.broadcast_to(energy, (UPDATE_CHUNK, 128)))[0:1]
    keep.wait()


def last_kernel(length_ref, total_ref, energy_ref, gain_ref, out_ref, width):
    rows = total_ref.shape[0]
    seq = place_in_seq()
    live = length_ref[seq // BR_SPAN] - (seq % BR_SPAN) * rows
    slot = lax.broadcasted_iota(jnp.int32, (1, rows), 1)
    inverse = jnp.where(slot < live, lax.rsqrt(energy_ref[...] / width + 1e-06), 0.0)
    columns = jnp.tile(column_of(inverse), (1, total_ref.shape[1] // 128))
    out_ref[...] = (total_ref[...] * columns * gain_ref[...]).astype(jnp.bfloat16)


def replicate_kernel(*refs):
    total = refs[0][...].astype(jnp.float32)
    for ref in refs[1:-1]:
        total = total + ref[...].astype(jnp.float32)
    total = total.astype(jnp.bfloat16)
    for slot in range(refs[-1].shape[0]):
        refs[-1][slot] = total


def plane_kernel(received_ref, mine_ref):
    mine_ref[...] = jnp.sum(received_ref[...].astype(jnp.float32), axis=0).astype(jnp.bfloat16)


SMEM = pl.BlockSpec(memory_space=pltpu.SMEM)
VMEM = pl.BlockSpec(memory_space=pltpu.VMEM)
HBM = pl.BlockSpec(memory_space=pltpu.HBM)


def call(kernel, scalars, arrays, outs, held=(), held_outs=(), scratch=(), flops=0, vmem=VMEM_BYTES):
    moved = sum(array.size * array.dtype.itemsize for array in (*arrays, *held, *outs, *held_outs))
    return pl.pallas_call(
        kernel,
        out_shape=(*outs, *held_outs),
        in_specs=[SMEM] * len(scalars) + [VMEM] * len(arrays) + [HBM] * len(held),
        out_specs=[VMEM] * len(outs) + [HBM] * len(held_outs),
        scratch_shapes=list(scratch),
        compiler_params=pltpu.CompilerParams(vmem_limit_bytes=vmem),
        cost_estimate=pl.CostEstimate(flops=flops, bytes_accessed=moved, transcendentals=0),
    )(*scalars, *arrays, *held)


def shape(dims, kind):
    return jax.ShapeDtypeStruct(dims, kind)


def space(dims, kind=jnp.bfloat16):
    return pltpu.VMEM(dims, kind)


def gradient_first(split, rates, weights, keys, values, parts_shape):
    scratch = (
        space(rates.shape, rates.dtype),
        space(weights.shape),
        space(keys.shape),
        space(values.shape),
        space(parts_shape.shape),
        pltpu.SemaphoreType.DMA((6,)),
        pltpu.SemaphoreType.DMA((3 * keys.shape[0] // CHUNK,)),
    )
    (parts,) = call(
        first_kernel,
        (split,),
        (),
        (),
        (rates, weights, keys, values),
        (parts_shape,),
        scratch,
        flops=12 * keys.size * weights.shape[1],
        vmem=WHOLE_VMEM,
    )
    return parts


def by_kind(gathered):
    planes, kinds, step, width = gathered.shape
    return space((kinds, planes, step, width))


def update_and_gradient(split, step, gathered, rates, weights, keys, values):
    full = weights.shape
    scratch = (
        space(rates.shape, rates.dtype),
        space(full),
        space(keys.shape),
        space(values.shape),
        space((2, *full)),
        space(full),
        space(full),
        by_kind(gathered),
        space(gathered.shape),
        pltpu.SemaphoreType.DMA((5,)),
        pltpu.SemaphoreType.DMA((3,)),
        pltpu.SemaphoreType.DMA((3 * full[1] // CHUNK,)),
    )
    return call(
        second_kernel,
        (split, step),
        (),
        (),
        (rates, gathered, weights, keys, values),
        (shape(gathered.shape, jnp.bfloat16), shape(full, jnp.bfloat16)),
        scratch,
        flops=48 * keys.size * full[1],
        vmem=SECOND_VMEM,
    )


def update_and_apply(split, forks, step, gathered, weights, state, query, attended, trunk_total):
    full = weights.shape
    rows, width = query.shape
    scratch = (
        space(full),
        space(query.shape),
        space((2, *full)),
        space(full),
        space((2, *full)),
        pltpu.SemaphoreType.DMA((4,)),
    )
    return call(
        functools.partial(third_kernel, trunk_total=trunk_total),
        (split, forks, step),
        (gathered, attended),
        (shape((rows, width), jnp.float32), shape((1, rows), jnp.float32)),
        (weights, state, query),
        (shape(full, jnp.bfloat16),),
        scratch,
        flops=42 * query.size * full[1],
        vmem=LAST_VMEM,
    )


def from_behind(value):
    count = lax.axis_size("z")
    return lax.ppermute(value, "z", [(source, source + 1) for source in range(count - 1)])


def sum_plane_in_kernel(parts):
    received = lax.all_to_all(parts, PLANE, 0, 0, tiled=False)
    (mine,) = call(plane_kernel, (), (received,), (shape(received.shape[1:], jnp.bfloat16),))
    return mine


def sum_plane(parts):
    received = lax.all_to_all(parts, PLANE, 0, 0, tiled=False)
    return jnp.sum(received.astype(jnp.float32), axis=0).astype(jnp.bfloat16)


def swap_depth(value, flip):
    depth = lax.axis_size("z")
    return lax.ppermute(value, "z", [(i, i ^ flip) for i in range(depth)])


def sum_depth(mine, beside=None):
    planes = lax.axis_size(PLANE)
    other, beside = lax.optimization_barrier((swap_depth(mine, 1), beside))
    pair = (mine.astype(jnp.float32) + other.astype(jnp.float32)).astype(jnp.bfloat16)
    (copies,) = call(
        replicate_kernel, (), (pair, swap_depth(pair, 3)), (shape((planes, *mine.shape), mine.dtype),)
    )
    return copies, beside


def spread_plane(copies):
    return lax.all_to_all(copies, PLANE, 0, 0, tiled=False)


def per_device(
    trunk_keys,
    trunk_values,
    trunk_rates,
    segment_end,
    fast_weights,
    step_sizes,
    branch_query,
    branch_keys,
    branch_values,
    branch_lengths,
    fork_points,
    out_gain,
):
    keys, values = trunk_keys[0], trunk_values[0]
    weights = fast_weights[:, 0]
    query, own_keys, own_values = branch_query[0], branch_keys[0], branch_values[0]
    rows, width = keys.shape
    hidden = weights.shape[1]
    planes = lax.axis_size(PLANE)
    trunk_total = rows * lax.axis_size(SEQ)
    total_width = width * lax.axis_size(HEAD)
    parts_shape = shape((planes, 3, hidden // planes, width), jnp.bfloat16)
    barrier = lax.optimization_barrier
    most = 3 * rows // 4

    keys_a = from_behind(own_keys[:most])
    parts = gradient_first(segment_end, trunk_rates, weights, keys, values, parts_shape)
    mine, keys_a = barrier((sum_plane(parts), keys_a))
    copies, _ = sum_depth(mine)
    copies, rest_keys, rest_values = barrier((copies, own_keys[most:], own_values[: rows - most]))
    gathered, keys_b, values_b = barrier((spread_plane(copies), from_behind(rest_keys), from_behind(rest_values)))
    parts, state = update_and_gradient(
        segment_end, step_sizes, gathered, trunk_rates, weights, keys, values
    )
    parts, rest_values = barrier((parts, own_values[rows - most :]))
    mine, values_c, query = barrier((sum_plane_in_kernel(parts), from_behind(rest_values), query))
    (attended,) = call(
        attend_kernel,
        (branch_lengths,),
        (query, own_keys, own_values, keys_a, keys_b, values_b, values_c),
        (shape((rows, width), jnp.float32),),
        flops=8 * rows * rows * width,
    )
    copies, attended = sum_depth(mine, attended)
    gathered = spread_plane(copies)
    total, energy, last = update_and_apply(
        segment_end, fork_points, step_sizes, gathered, weights, state, query, attended, trunk_total
    )
    energy = lax.psum(energy, HEAD)
    (result,) = call(
        functools.partial(last_kernel, width=total_width),
        (branch_lengths,),
        (total, energy, out_gain),
        (shape((rows, width), jnp.bfloat16),),
    )
    return (result[None], last[:, None])


def solution(mesh):
    fine = Mesh(mesh.devices.reshape(4, 4, 4, 2, 2), (*SEQ, *HEAD))
    rows = P(HEAD, SEQ, None)
    placed = (
        rows,
        rows,
        P(HEAD, SEQ),
        P(),
        P(None, HEAD, None, None),
        P(HEAD),
        rows,
        rows,
        rows,
        P(),
        P(),
        P(HEAD, None),
    )
    return jax.shard_map(
        per_device,
        mesh=fine,
        in_specs=placed,
        out_specs=(rows, P(None, HEAD, None, None)),
        check_vma=False,
    )
```

```python
import functools
import jax
import jax.numpy as jnp
from jax import lax
from jax.experimental import pallas as pl
from jax.experimental.pallas import tpu as pltpu
from jax.sharding import Mesh
from jax.sharding import PartitionSpec as P

PLANE = ("x", "y")
SEQ = ("x", "y", "z")
HEAD = ("w", "c")
NS_STEPS = 2
BR_SPAN = 4

poly_one = 3.4445
poly_two = -4.775
poly_three = 2.0315
VMEM_BYTES = 24 * 1024 * 1024
WHOLE_VMEM = 60 * 1024 * 1024
LAST_VMEM = 46 * 1024 * 1024
SECOND_VMEM = 61 * 1024 * 1024
CHUNK = 256
UPDATE_CHUNK = 512


def nt(left, right):
    return lax.dot_general(left, right, (((1,), (1,)), ((), ())), preferred_element_type=jnp.float32)


def nn(left, right):
    return jnp.dot(left, right, preferred_element_type=jnp.float32)


def column_of(row):
    return jnp.transpose(jnp.broadcast_to(row, (128, row.shape[1])))


def emit_gradient(weights, keys_ref, values_ref, rates, parts_ref, parts_hbm, sems, ready=lambda name: None):
    step = parts_ref.shape[2]
    sent = []
    rows, width = weights[0].shape
    ready("keys")
    keys = keys_ref[...]
    pushed = None
    for start in range(0, rows, CHUNK):
        cut = slice(start, start + CHUNK)
        if start == 0:
            ready("first")
        first = nt(weights[0][cut], keys)
        if start == 0:
            ready("third")
        third = nt(weights[1][cut], keys)
        gate = jax.nn.sigmoid(first)
        silu = first * gate
        hidden = (silu * third).astype(jnp.bfloat16)
        if start == 0:
            ready("rates")
            rate_columns = jnp.tile(column_of(rates()), (1, width // 128))
            ready("values")
            pushed = (rate_columns * values_ref[...].astype(jnp.float32)).astype(jnp.bfloat16)
            ready("second")
        returned = nt(weights[2][cut], pushed)
        delta_first = (returned * third * gate * (1.0 + first * (1.0 - gate))).astype(jnp.bfloat16)
        delta_third = (returned * silu).astype(jnp.bfloat16)
        for kind, grad in enumerate((nn(delta_first, keys), nn(delta_third, keys), nn(hidden, pushed))):
            grad = grad.astype(jnp.bfloat16)
            for part in range(CHUNK // step):
                parts_ref[start // step + part, kind] = grad[part * step : (part + 1) * step]
            slots = pl.ds(start // step, CHUNK // step)
            copy = pltpu.make_async_copy(
                parts_ref.at[slots, kind], parts_hbm.at[slots, kind], sems.at[len(sent)]
            )
            copy.start()
            sent.append(copy)
    for copy in sent:
        copy.wait()


def fetch_gathered(gathered_hbm, gathered_ref, sems):
    copies = [
        pltpu.make_async_copy(gathered_hbm.at[:, kind], gathered_ref.at[kind], sems.at[kind])
        for kind in range(gathered_ref.shape[0])
    ]
    for copy in copies:
        copy.start()
    return copies


def emit_update(load, old_ref, step_size, x_ref, gram_ref, out_ref, begin, ready):
    kinds, rows, width = out_ref.shape
    for kind in range(kinds):
        wide = load(kind).reshape(rows, width).astype(jnp.float32)
        square = jnp.sum(jnp.sum(wide * wide, axis=0, keepdims=True), axis=1, keepdims=True)
        inverse = 1.0 / (jnp.sqrt(square) + 1e-07)
        x_ref[0, kind] = (wide * inverse).astype(jnp.bfloat16)
    begin()
    for sweep in range(NS_STEPS):
        now, later = sweep % 2, (sweep + 1) % 2
        if sweep == NS_STEPS - 1:
            ready()
        for kind in range(kinds):
            full = x_ref[now, kind]
            gram_ref[kind] = nt(full, full).astype(jnp.bfloat16)
        for kind in range(kinds):
            full = x_ref[now, kind]
            gram = gram_ref[kind]
            for start in range(0, rows, UPDATE_CHUNK):
                cut = slice(start, start + UPDATE_CHUNK)
                own = gram[cut]
                poly = (poly_two * own.astype(jnp.float32) + poly_three * nn(own, gram)).astype(jnp.bfloat16)
                moved = (poly_one * full[cut].astype(jnp.float32) + nn(poly, full)).astype(jnp.bfloat16)
                if sweep < NS_STEPS - 1:
                    x_ref[later, kind, cut] = moved
                else:
                    old = old_ref[kind, cut].astype(jnp.float32)
                    new = old + step_size * moved.astype(jnp.float32)
                    old_mean = jnp.mean(old * old, axis=-1, keepdims=True) + 1e-06
                    new_mean = jnp.mean(new * new, axis=-1, keepdims=True) + 1e-06
                    out_ref[kind, cut] = (new * (jnp.sqrt(old_mean) * lax.rsqrt(new_mean))).astype(jnp.bfloat16)


def place_in_seq():
    return lax.axis_index(SEQ).astype(jnp.int32)


def masked_rates(rates, split_ref, period):
    count = rates.shape[1]
    positions = place_in_seq() * count + lax.broadcasted_iota(jnp.int32, rates.shape, 1)
    early = positions < split_ref[0]
    return jnp.where(early if period == 0 else jnp.logical_not(early), rates, 0.0)


def first_kernel(
    split_ref,
    rates_hbm,
    weights_hbm,
    keys_hbm,
    values_hbm,
    parts_hbm,
    rates,
    weights,
    keys,
    values,
    parts,
    sems,
    parts_sems,
):
    copies = {
        "keys": pltpu.make_async_copy(keys_hbm, keys, sems.at[0]),
        "first": pltpu.make_async_copy(weights_hbm.at[0], weights.at[0], sems.at[1]),
        "third": pltpu.make_async_copy(weights_hbm.at[1], weights.at[1], sems.at[2]),
        "values": pltpu.make_async_copy(values_hbm, values, sems.at[3]),
        "second": pltpu.make_async_copy(weights_hbm.at[2], weights.at[2], sems.at[4]),
        "rates": pltpu.make_async_copy(rates_hbm, rates, sems.at[5]),
    }
    for copy in copies.values():
        copy.start()
    kinds = [weights.at[kind] for kind in range(3)]
    emit_gradient(kinds, keys, values, lambda: masked_rates(rates[...], split_ref, 0), parts, parts_hbm, parts_sems, lambda name: copies[name].wait())


def second_kernel(
    split_ref,
    step_ref,
    rates_hbm,
    gathered_hbm,
    weights_hbm,
    keys_hbm,
    values_hbm,
    parts_hbm,
    state_hbm,
    rates,
    weights,
    keys,
    values,
    x_ref,
    gram_ref,
    state,
    gathered,
    parts,
    sems,
    gathered_sems,
    parts_sems,
):
    fetches = fetch_gathered(gathered_hbm, gathered, gathered_sems)
    fetch_weights = pltpu.make_async_copy(weights_hbm, weights, sems.at[0])
    fetch_keys = pltpu.make_async_copy(keys_hbm, keys, sems.at[1])
    fetch_values = pltpu.make_async_copy(values_hbm, values, sems.at[2])
    fetch_rates = pltpu.make_async_copy(rates_hbm, rates, sems.at[4])

    def begin():
        fetch_weights.start()
        fetch_keys.start()
        fetch_values.start()
        fetch_rates.start()

    def load(kind):
        fetches[kind].wait()
        return gathered[kind]

    emit_update(load, weights, step_ref[0], x_ref, gram_ref, state, begin, fetch_weights.wait)
    keep = pltpu.make_async_copy(state, state_hbm, sems.at[3])
    keep.start()
    fetch_keys.wait()
    fetch_values.wait()
    fetch_rates.wait()
    kinds = [state.at[kind] for kind in range(3)]
    emit_gradient(kinds, keys, values, lambda: masked_rates(rates[...], split_ref, 1), parts, parts_hbm, parts_sems)
    keep.wait()


def attend_kernel(
    length_ref, query_ref, keys_ref, values_ref, keys_a_ref, keys_b_ref, values_b_ref, values_c_ref, out_ref
):
    rows, width = query_ref.shape
    seq = place_in_seq()
    branch = seq // BR_SPAN
    place = seq % BR_SPAN
    live = length_ref[branch] - place * rows
    scale = width ** (-0.5)
    prior_keys = jnp.concatenate([keys_a_ref[...], keys_b_ref[...]], axis=0)
    prior_values = jnp.concatenate([values_b_ref[...], values_c_ref[...]], axis=0)
    chunk = 128
    for start in range(0, rows, chunk):
        cut = slice(start, start + chunk)
        query = query_ref[cut]
        row = start + lax.broadcasted_iota(jnp.int32, (chunk, rows), 0)
        slot = lax.broadcasted_iota(jnp.int32, (chunk, rows), 1)
        behind = slot > row
        allowed = (slot == row) | (slot < jnp.where(behind, jnp.where(place > 0, rows, 0), live))
        scores = jnp.where(behind, nt(query, prior_keys), nt(query, keys_ref[...])) * scale
        scores = jnp.where(allowed, scores, -1e30)
        top = jnp.max(scores, axis=-1, keepdims=True)
        power = jnp.exp(scores - top)
        share = power * (1.0 / jnp.sum(power, axis=-1, keepdims=True))
        out_ref[cut] = nn(jnp.where(behind, share, 0.0).astype(jnp.bfloat16), prior_values) + nn(
            jnp.where(behind, 0.0, share).astype(jnp.bfloat16), values_ref[...]
        )


def third_kernel(
    split_ref,
    fork_ref,
    step_ref,
    gathered_ref,
    attended_ref,
    weights_hbm,
    state_hbm,
    query_hbm,
    total_ref,
    energy_ref,
    last_hbm,
    old,
    query,
    x_ref,
    gram_ref,
    pool,
    sems,
    trunk_total,
):
    fork = fork_ref[place_in_seq() // BR_SPAN]
    early = fork < split_ref[0]
    final = jnp.logical_and(jnp.logical_not(early), fork >= trunk_total)
    fetch_old = pltpu.make_async_copy(state_hbm, old, sems.at[0])
    fetch_query = pltpu.make_async_copy(query_hbm, query, sems.at[1])
    fetch_first = pltpu.make_async_copy(weights_hbm, pool.at[1], sems.at[2])
    fetch_state = pltpu.make_async_copy(state_hbm, pool.at[1], sems.at[2])

    def begin():
        fetch_old.start()
        fetch_query.start()

        @pl.when(early)
        def _():
            fetch_first.start()

        @pl.when(jnp.logical_not(early))
        def _():
            fetch_state.start()

    emit_update(lambda kind: gathered_ref[:, kind], old, step_ref[0], x_ref, gram_ref, pool.at[0], begin, fetch_old.wait)
    keep = pltpu.make_async_copy(pool.at[0], last_hbm, sems.at[3])
    keep.start()
    fetch_query.wait()
    fetch_state.wait()
    pick = jnp.where(final, 0, 1)
    rows = query.shape[0]
    for start in range(0, rows, UPDATE_CHUNK):
        cut = slice(start, start + UPDATE_CHUNK)
        first = nt(query[cut], pool[pick, 0])
        third = nt(query[cut], pool[pick, 1])
        hidden = (first * jax.nn.sigmoid(first) * third).astype(jnp.bfloat16)
        total = attended_ref[cut] + nn(hidden, pool[pick, 2])
        total_ref[cut] = total
        energy = jnp.sum(total * total, axis=-1, keepdims=True)
        energy_ref[:, cut] = jnp.transpose(jnp.broadcast_to(energy, (UPDATE_CHUNK, 128)))[0:1]
    keep.wait()


def last_kernel(length_ref, total_ref, energy_ref, gain_ref, out_ref, width):
    rows = total_ref.shape[0]
    seq = place_in_seq()
    live = length_ref[seq // BR_SPAN] - (seq % BR_SPAN) * rows
    slot = lax.broadcasted_iota(jnp.int32, (1, rows), 1)
    inverse = jnp.where(slot < live, lax.rsqrt(energy_ref[...] / width + 1e-06), 0.0)
    columns = jnp.tile(column_of(inverse), (1, total_ref.shape[1] // 128))
    out_ref[...] = (total_ref[...] * columns * gain_ref[...]).astype(jnp.bfloat16)


def replicate_kernel(*refs):
    total = refs[0][...].astype(jnp.float32)
    for ref in refs[1:-1]:
        total = total + ref[...].astype(jnp.float32)
    total = total.astype(jnp.bfloat16)
    for slot in range(refs[-1].shape[0]):
        refs[-1][slot] = total


def plane_kernel(received_ref, mine_ref):
    mine_ref[...] = jnp.sum(received_ref[...].astype(jnp.float32), axis=0).astype(jnp.bfloat16)


SMEM = pl.BlockSpec(memory_space=pltpu.SMEM)
VMEM = pl.BlockSpec(memory_space=pltpu.VMEM)
HBM = pl.BlockSpec(memory_space=pltpu.HBM)


def call(kernel, scalars, arrays, outs, held=(), held_outs=(), scratch=(), flops=0, vmem=VMEM_BYTES):
    moved = sum(array.size * array.dtype.itemsize for array in (*arrays, *held, *outs, *held_outs))
    return pl.pallas_call(
        kernel,
        out_shape=(*outs, *held_outs),
        in_specs=[SMEM] * len(scalars) + [VMEM] * len(arrays) + [HBM] * len(held),
        out_specs=[VMEM] * len(outs) + [HBM] * len(held_outs),
        scratch_shapes=list(scratch),
        compiler_params=pltpu.CompilerParams(vmem_limit_bytes=vmem),
        cost_estimate=pl.CostEstimate(flops=flops, bytes_accessed=moved, transcendentals=0),
    )(*scalars, *arrays, *held)


def shape(dims, kind):
    return jax.ShapeDtypeStruct(dims, kind)


def space(dims, kind=jnp.bfloat16):
    return pltpu.VMEM(dims, kind)


def gradient_first(split, rates, weights, keys, values, parts_shape):
    scratch = (
        space(rates.shape, rates.dtype),
        space(weights.shape),
        space(keys.shape),
        space(values.shape),
        space(parts_shape.shape),
        pltpu.SemaphoreType.DMA((6,)),
        pltpu.SemaphoreType.DMA((3 * keys.shape[0] // CHUNK,)),
    )
    (parts,) = call(
        first_kernel,
        (split,),
        (),
        (),
        (rates, weights, keys, values),
        (parts_shape,),
        scratch,
        flops=12 * keys.size * weights.shape[1],
        vmem=WHOLE_VMEM,
    )
    return parts


def by_kind(gathered):
    planes, kinds, step, width = gathered.shape
    return space((kinds, planes, step, width))


def update_and_gradient(split, step, gathered, rates, weights, keys, values):
    full = weights.shape
    scratch = (
        space(rates.shape, rates.dtype),
        space(full),
        space(keys.shape),
        space(values.shape),
        space((2, *full)),
        space(full),
        space(full),
        by_kind(gathered),
        space(gathered.shape),
        pltpu.SemaphoreType.DMA((5,)),
        pltpu.SemaphoreType.DMA((3,)),
        pltpu.SemaphoreType.DMA((3 * full[1] // CHUNK,)),
    )
    return call(
        second_kernel,
        (split, step),
        (),
        (),
        (rates, gathered, weights, keys, values),
        (shape(gathered.shape, jnp.bfloat16), shape(full, jnp.bfloat16)),
        scratch,
        flops=48 * keys.size * full[1],
        vmem=SECOND_VMEM,
    )


def update_and_apply(split, forks, step, gathered, weights, state, query, attended, trunk_total):
    full = weights.shape
    rows, width = query.shape
    scratch = (
        space(full),
        space(query.shape),
        space((2, *full)),
        space(full),
        space((2, *full)),
        pltpu.SemaphoreType.DMA((4,)),
    )
    return call(
        functools.partial(third_kernel, trunk_total=trunk_total),
        (split, forks, step),
        (gathered, attended),
        (shape((rows, width), jnp.float32), shape((1, rows), jnp.float32)),
        (weights, state, query),
        (shape(full, jnp.bfloat16),),
        scratch,
        flops=42 * query.size * full[1],
        vmem=LAST_VMEM,
    )


def from_behind(value):
    count = lax.axis_size("z")
    return lax.ppermute(value, "z", [(source, source + 1) for source in range(count - 1)])


def sum_plane_in_kernel(parts):
    received = lax.all_to_all(parts, PLANE, 0, 0, tiled=False)
    (mine,) = call(plane_kernel, (), (received,), (shape(received.shape[1:], jnp.bfloat16),))
    return mine


def sum_plane(parts):
    received = lax.all_to_all(parts, PLANE, 0, 0, tiled=False)
    return jnp.sum(received.astype(jnp.float32), axis=0).astype(jnp.bfloat16)


def swap_depth(value, flip):
    depth = lax.axis_size("z")
    return lax.ppermute(value, "z", [(i, i ^ flip) for i in range(depth)])


def sum_depth(mine, beside=None):
    planes = lax.axis_size(PLANE)
    other, beside = lax.optimization_barrier((swap_depth(mine, 1), beside))
    pair = (mine.astype(jnp.float32) + other.astype(jnp.float32)).astype(jnp.bfloat16)
    (copies,) = call(
        replicate_kernel, (), (pair, swap_depth(pair, 3)), (shape((planes, *mine.shape), mine.dtype),)
    )
    return copies, beside


def spread_plane(copies):
    return lax.all_to_all(copies, PLANE, 0, 0, tiled=False)


def per_device(
    trunk_keys,
    trunk_values,
    trunk_rates,
    segment_end,
    fast_weights,
    step_sizes,
    branch_query,
    branch_keys,
    branch_values,
    branch_lengths,
    fork_points,
    out_gain,
):
    keys, values = trunk_keys[0], trunk_values[0]
    weights = fast_weights[:, 0]
    query, own_keys, own_values = branch_query[0], branch_keys[0], branch_values[0]
    rows, width = keys.shape
    hidden = weights.shape[1]
    planes = lax.axis_size(PLANE)
    trunk_total = rows * lax.axis_size(SEQ)
    total_width = width * lax.axis_size(HEAD)
    parts_shape = shape((planes, 3, hidden // planes, width), jnp.bfloat16)
    barrier = lax.optimization_barrier
    most, few = 5 * rows // 8, rows // 4

    keys_a = from_behind(own_keys[:most])
    parts = gradient_first(segment_end, trunk_rates, weights, keys, values, parts_shape)
    mine, keys_a = barrier((sum_plane_in_kernel(parts), keys_a))
    copies, _ = sum_depth(mine)
    copies, rest_keys, rest_values = barrier((copies, own_keys[most:], own_values[:few]))
    gathered, keys_b, values_b = barrier((spread_plane(copies), from_behind(rest_keys), from_behind(rest_values)))
    parts, state = update_and_gradient(
        segment_end, step_sizes, gathered, trunk_rates, weights, keys, values
    )
    parts, rest_values = barrier((parts, own_values[few:]))
    mine, values_c, query = barrier((sum_plane_in_kernel(parts), from_behind(rest_values), query))
    (attended,) = call(
        attend_kernel,
        (branch_lengths,),
        (query, own_keys, own_values, keys_a, keys_b, values_b, values_c),
        (shape((rows, width), jnp.float32),),
        flops=8 * rows * rows * width,
    )
    copies, attended = sum_depth(mine, attended)
    gathered = spread_plane(copies)
    total, energy, last = update_and_apply(
        segment_end, fork_points, step_sizes, gathered, weights, state, query, attended, trunk_total
    )
    energy = lax.psum(energy, HEAD)
    (result,) = call(
        functools.partial(last_kernel, width=total_width),
        (branch_lengths,),
        (total, energy, out_gain),
        (shape((rows, width), jnp.bfloat16),),
    )
    return (result[None], last[:, None])


def solution(mesh):
    fine = Mesh(mesh.devices.reshape(4, 4, 4, 2, 2), (*SEQ, *HEAD))
    rows = P(HEAD, SEQ, None)
    placed = (
        rows,
        rows,
        P(HEAD, SEQ),
        P(),
        P(None, HEAD, None, None),
        P(HEAD),
        rows,
        rows,
        rows,
        P(),
        P(),
        P(HEAD, None),
    )
    return jax.shard_map(
        per_device,
        mesh=fine,
        in_specs=placed,
        out_specs=(rows, P(None, HEAD, None, None)),
        check_vma=False,
    )
```

```python
import functools
import jax
import jax.numpy as jnp
from jax import lax
from jax.experimental import pallas as pl
from jax.experimental.pallas import tpu as pltpu
from jax.sharding import Mesh
from jax.sharding import PartitionSpec as P

PLANE = ("x", "y")
SEQ = ("x", "y", "z")
HEAD = ("w", "c")
NS_STEPS = 2
BR_SPAN = 4

poly_one = 3.4445
poly_two = -4.775
poly_three = 2.0315
VMEM_BYTES = 24 * 1024 * 1024
WHOLE_VMEM = 60 * 1024 * 1024
LAST_VMEM = 46 * 1024 * 1024
SECOND_VMEM = 61 * 1024 * 1024
CHUNK = 256
UPDATE_CHUNK = 512


def nt(left, right):
    return lax.dot_general(left, right, (((1,), (1,)), ((), ())), preferred_element_type=jnp.float32)


def nn(left, right):
    return jnp.dot(left, right, preferred_element_type=jnp.float32)


def column_of(row):
    return jnp.transpose(jnp.broadcast_to(row, (128, row.shape[1])))


def emit_gradient(weights, keys_ref, values_ref, rates, parts_ref, parts_hbm, sems, ready=lambda name: None):
    step = parts_ref.shape[2]
    sent = []
    rows, width = weights[0].shape
    ready("keys")
    keys = keys_ref[...]
    pushed = None
    for start in range(0, rows, CHUNK):
        cut = slice(start, start + CHUNK)
        if start == 0:
            ready("first")
        first = nt(weights[0][cut], keys)
        if start == 0:
            ready("third")
        third = nt(weights[1][cut], keys)
        gate = jax.nn.sigmoid(first)
        silu = first * gate
        hidden = (silu * third).astype(jnp.bfloat16)
        if start == 0:
            ready("rates")
            rate_columns = jnp.tile(column_of(rates()), (1, width // 128))
            ready("values")
            pushed = (rate_columns * values_ref[...].astype(jnp.float32)).astype(jnp.bfloat16)
            ready("second")
        returned = nt(weights[2][cut], pushed)
        delta_first = (returned * third * gate * (1.0 + first * (1.0 - gate))).astype(jnp.bfloat16)
        delta_third = (returned * silu).astype(jnp.bfloat16)
        for kind, grad in enumerate((nn(delta_first, keys), nn(delta_third, keys), nn(hidden, pushed))):
            grad = grad.astype(jnp.bfloat16)
            for part in range(CHUNK // step):
                parts_ref[start // step + part, kind] = grad[part * step : (part + 1) * step]
            slots = pl.ds(start // step, CHUNK // step)
            copy = pltpu.make_async_copy(
                parts_ref.at[slots, kind], parts_hbm.at[slots, kind], sems.at[len(sent)]
            )
            copy.start()
            sent.append(copy)
    for copy in sent:
        copy.wait()


def fetch_gathered(gathered_hbm, gathered_ref, sems):
    copies = [
        pltpu.make_async_copy(gathered_hbm.at[:, kind], gathered_ref.at[kind], sems.at[kind])
        for kind in range(gathered_ref.shape[0])
    ]
    for copy in copies:
        copy.start()
    return copies


def emit_update(load, old_ref, step_size, x_ref, gram_ref, out_ref, begin, ready):
    kinds, rows, width = out_ref.shape
    for kind in range(kinds):
        wide = load(kind).reshape(rows, width).astype(jnp.float32)
        square = jnp.sum(jnp.sum(wide * wide, axis=0, keepdims=True), axis=1, keepdims=True)
        inverse = 1.0 / (jnp.sqrt(square) + 1e-07)
        x_ref[0, kind] = (wide * inverse).astype(jnp.bfloat16)
    begin()
    for sweep in range(NS_STEPS):
        now, later = sweep % 2, (sweep + 1) % 2
        if sweep == NS_STEPS - 1:
            ready()
        for kind in range(kinds):
            full = x_ref[now, kind]
            gram_ref[kind] = nt(full, full).astype(jnp.bfloat16)
        for kind in range(kinds):
            full = x_ref[now, kind]
            gram = gram_ref[kind]
            for start in range(0, rows, UPDATE_CHUNK):
                cut = slice(start, start + UPDATE_CHUNK)
                own = gram[cut]
                poly = (poly_two * own.astype(jnp.float32) + poly_three * nn(own, gram)).astype(jnp.bfloat16)
                moved = (poly_one * full[cut].astype(jnp.float32) + nn(poly, full)).astype(jnp.bfloat16)
                if sweep < NS_STEPS - 1:
                    x_ref[later, kind, cut] = moved
                else:
                    old = old_ref[kind, cut].astype(jnp.float32)
                    new = old + step_size * moved.astype(jnp.float32)
                    old_mean = jnp.mean(old * old, axis=-1, keepdims=True) + 1e-06
                    new_mean = jnp.mean(new * new, axis=-1, keepdims=True) + 1e-06
                    out_ref[kind, cut] = (new * (jnp.sqrt(old_mean) * lax.rsqrt(new_mean))).astype(jnp.bfloat16)


def place_in_seq():
    return lax.axis_index(SEQ).astype(jnp.int32)


def masked_rates(rates, split_ref, period):
    count = rates.shape[1]
    positions = place_in_seq() * count + lax.broadcasted_iota(jnp.int32, rates.shape, 1)
    early = positions < split_ref[0]
    return jnp.where(early if period == 0 else jnp.logical_not(early), rates, 0.0)


def first_kernel(
    split_ref,
    rates_hbm,
    weights_hbm,
    keys_hbm,
    values_hbm,
    parts_hbm,
    rates,
    weights,
    keys,
    values,
    parts,
    sems,
    parts_sems,
):
    copies = {
        "keys": pltpu.make_async_copy(keys_hbm, keys, sems.at[0]),
        "first": pltpu.make_async_copy(weights_hbm.at[0], weights.at[0], sems.at[1]),
        "third": pltpu.make_async_copy(weights_hbm.at[1], weights.at[1], sems.at[2]),
        "values": pltpu.make_async_copy(values_hbm, values, sems.at[3]),
        "second": pltpu.make_async_copy(weights_hbm.at[2], weights.at[2], sems.at[4]),
        "rates": pltpu.make_async_copy(rates_hbm, rates, sems.at[5]),
    }
    for copy in copies.values():
        copy.start()
    kinds = [weights.at[kind] for kind in range(3)]
    emit_gradient(kinds, keys, values, lambda: masked_rates(rates[...], split_ref, 0), parts, parts_hbm, parts_sems, lambda name: copies[name].wait())


def second_kernel(
    split_ref,
    step_ref,
    rates_hbm,
    gathered_hbm,
    weights_hbm,
    keys_hbm,
    values_hbm,
    parts_hbm,
    state_hbm,
    rates,
    weights,
    keys,
    values,
    x_ref,
    gram_ref,
    state,
    gathered,
    parts,
    sems,
    gathered_sems,
    parts_sems,
):
    fetches = fetch_gathered(gathered_hbm, gathered, gathered_sems)
    fetch_weights = pltpu.make_async_copy(weights_hbm, weights, sems.at[0])
    fetch_keys = pltpu.make_async_copy(keys_hbm, keys, sems.at[1])
    fetch_values = pltpu.make_async_copy(values_hbm, values, sems.at[2])
    fetch_rates = pltpu.make_async_copy(rates_hbm, rates, sems.at[4])

    def begin():
        fetch_weights.start()
        fetch_keys.start()
        fetch_values.start()
        fetch_rates.start()

    def load(kind):
        fetches[kind].wait()
        return gathered[kind]

    emit_update(load, weights, step_ref[0], x_ref, gram_ref, state, begin, fetch_weights.wait)
    keep = pltpu.make_async_copy(state, state_hbm, sems.at[3])
    keep.start()
    fetch_keys.wait()
    fetch_values.wait()
    fetch_rates.wait()
    kinds = [state.at[kind] for kind in range(3)]
    emit_gradient(kinds, keys, values, lambda: masked_rates(rates[...], split_ref, 1), parts, parts_hbm, parts_sems)
    keep.wait()


def attend_kernel(
    length_ref, query_ref, keys_ref, values_ref, keys_a_ref, keys_b_ref, values_b_ref, values_c_ref, out_ref
):
    rows, width = query_ref.shape
    seq = place_in_seq()
    branch = seq // BR_SPAN
    place = seq % BR_SPAN
    live = length_ref[branch] - place * rows
    scale = width ** (-0.5)
    prior_keys = jnp.concatenate([keys_a_ref[...], keys_b_ref[...]], axis=0)
    prior_values = jnp.concatenate([values_b_ref[...], values_c_ref[...]], axis=0)
    chunk = 128
    for start in range(0, rows, chunk):
        cut = slice(start, start + chunk)
        query = query_ref[cut]
        row = start + lax.broadcasted_iota(jnp.int32, (chunk, rows), 0)
        slot = lax.broadcasted_iota(jnp.int32, (chunk, rows), 1)
        behind = slot > row
        allowed = (slot == row) | (slot < jnp.where(behind, jnp.where(place > 0, rows, 0), live))
        scores = jnp.where(behind, nt(query, prior_keys), nt(query, keys_ref[...])) * scale
        scores = jnp.where(allowed, scores, -1e30)
        top = jnp.max(scores, axis=-1, keepdims=True)
        power = jnp.exp(scores - top)
        share = power * (1.0 / jnp.sum(power, axis=-1, keepdims=True))
        out_ref[cut] = nn(jnp.where(behind, share, 0.0).astype(jnp.bfloat16), prior_values) + nn(
            jnp.where(behind, 0.0, share).astype(jnp.bfloat16), values_ref[...]
        )


def third_kernel(
    split_ref,
    fork_ref,
    step_ref,
    gathered_ref,
    attended_ref,
    weights_hbm,
    state_hbm,
    query_hbm,
    total_ref,
    energy_ref,
    last_hbm,
    old,
    query,
    x_ref,
    gram_ref,
    pool,
    sems,
    trunk_total,
):
    fork = fork_ref[place_in_seq() // BR_SPAN]
    early = fork < split_ref[0]
    final = jnp.logical_and(jnp.logical_not(early), fork >= trunk_total)
    fetch_old = pltpu.make_async_copy(state_hbm, old, sems.at[0])
    fetch_query = pltpu.make_async_copy(query_hbm, query, sems.at[1])
    fetch_first = pltpu.make_async_copy(weights_hbm, pool.at[1], sems.at[2])
    fetch_state = pltpu.make_async_copy(state_hbm, pool.at[1], sems.at[2])

    def begin():
        fetch_old.start()
        fetch_query.start()

        @pl.when(early)
        def _():
            fetch_first.start()

        @pl.when(jnp.logical_not(early))
        def _():
            fetch_state.start()

    emit_update(lambda kind: gathered_ref[:, kind], old, step_ref[0], x_ref, gram_ref, pool.at[0], begin, fetch_old.wait)
    keep = pltpu.make_async_copy(pool.at[0], last_hbm, sems.at[3])
    keep.start()
    fetch_query.wait()
    fetch_state.wait()
    pick = jnp.where(final, 0, 1)
    rows = query.shape[0]
    for start in range(0, rows, UPDATE_CHUNK):
        cut = slice(start, start + UPDATE_CHUNK)
        first = nt(query[cut], pool[pick, 0])
        third = nt(query[cut], pool[pick, 1])
        hidden = (first * jax.nn.sigmoid(first) * third).astype(jnp.bfloat16)
        total = attended_ref[cut] + nn(hidden, pool[pick, 2])
        total_ref[cut] = total
        energy = jnp.sum(total * total, axis=-1, keepdims=True)
        energy_ref[:, cut] = jnp.transpose(jnp.broadcast_to(energy, (UPDATE_CHUNK, 128)))[0:1]
    keep.wait()


def last_kernel(length_ref, total_ref, energy_ref, gain_ref, out_ref, width):
    rows = total_ref.shape[0]
    seq = place_in_seq()
    live = length_ref[seq // BR_SPAN] - (seq % BR_SPAN) * rows
    slot = lax.broadcasted_iota(jnp.int32, (1, rows), 1)
    inverse = jnp.where(slot < live, lax.rsqrt(energy_ref[...] / width + 1e-06), 0.0)
    columns = jnp.tile(column_of(inverse), (1, total_ref.shape[1] // 128))
    out_ref[...] = (total_ref[...] * columns * gain_ref[...]).astype(jnp.bfloat16)


def replicate_kernel(*refs):
    total = refs[0][...].astype(jnp.float32)
    for ref in refs[1:-1]:
        total = total + ref[...].astype(jnp.float32)
    total = total.astype(jnp.bfloat16)
    for slot in range(refs[-1].shape[0]):
        refs[-1][slot] = total


def plane_kernel(received_ref, mine_ref):
    mine_ref[...] = jnp.sum(received_ref[...].astype(jnp.float32), axis=0).astype(jnp.bfloat16)


SMEM = pl.BlockSpec(memory_space=pltpu.SMEM)
VMEM = pl.BlockSpec(memory_space=pltpu.VMEM)
HBM = pl.BlockSpec(memory_space=pltpu.HBM)


def call(kernel, scalars, arrays, outs, held=(), held_outs=(), scratch=(), flops=0, vmem=VMEM_BYTES):
    moved = sum(array.size * array.dtype.itemsize for array in (*arrays, *held, *outs, *held_outs))
    return pl.pallas_call(
        kernel,
        out_shape=(*outs, *held_outs),
        in_specs=[SMEM] * len(scalars) + [VMEM] * len(arrays) + [HBM] * len(held),
        out_specs=[VMEM] * len(outs) + [HBM] * len(held_outs),
        scratch_shapes=list(scratch),
        compiler_params=pltpu.CompilerParams(vmem_limit_bytes=vmem),
        cost_estimate=pl.CostEstimate(flops=flops, bytes_accessed=moved, transcendentals=0),
    )(*scalars, *arrays, *held)


def shape(dims, kind):
    return jax.ShapeDtypeStruct(dims, kind)


def space(dims, kind=jnp.bfloat16):
    return pltpu.VMEM(dims, kind)


def gradient_first(split, rates, weights, keys, values, parts_shape):
    scratch = (
        space(rates.shape, rates.dtype),
        space(weights.shape),
        space(keys.shape),
        space(values.shape),
        space(parts_shape.shape),
        pltpu.SemaphoreType.DMA((6,)),
        pltpu.SemaphoreType.DMA((3 * keys.shape[0] // CHUNK,)),
    )
    (parts,) = call(
        first_kernel,
        (split,),
        (),
        (),
        (rates, weights, keys, values),
        (parts_shape,),
        scratch,
        flops=12 * keys.size * weights.shape[1],
        vmem=WHOLE_VMEM,
    )
    return parts


def by_kind(gathered):
    planes, kinds, step, width = gathered.shape
    return space((kinds, planes, step, width))


def update_and_gradient(split, step, gathered, rates, weights, keys, values):
    full = weights.shape
    scratch = (
        space(rates.shape, rates.dtype),
        space(full),
        space(keys.shape),
        space(values.shape),
        space((2, *full)),
        space(full),
        space(full),
        by_kind(gathered),
        space(gathered.shape),
        pltpu.SemaphoreType.DMA((5,)),
        pltpu.SemaphoreType.DMA((3,)),
        pltpu.SemaphoreType.DMA((3 * full[1] // CHUNK,)),
    )
    return call(
        second_kernel,
        (split, step),
        (),
        (),
        (rates, gathered, weights, keys, values),
        (shape(gathered.shape, jnp.bfloat16), shape(full, jnp.bfloat16)),
        scratch,
        flops=48 * keys.size * full[1],
        vmem=SECOND_VMEM,
    )


def update_and_apply(split, forks, step, gathered, weights, state, query, attended, trunk_total):
    full = weights.shape
    rows, width = query.shape
    scratch = (
        space(full),
        space(query.shape),
        space((2, *full)),
        space(full),
        space((2, *full)),
        pltpu.SemaphoreType.DMA((4,)),
    )
    return call(
        functools.partial(third_kernel, trunk_total=trunk_total),
        (split, forks, step),
        (gathered, attended),
        (shape((rows, width), jnp.float32), shape((1, rows), jnp.float32)),
        (weights, state, query),
        (shape(full, jnp.bfloat16),),
        scratch,
        flops=42 * query.size * full[1],
        vmem=LAST_VMEM,
    )


def from_behind(value):
    count = lax.axis_size("z")
    return lax.ppermute(value, "z", [(source, source + 1) for source in range(count - 1)])


def sum_plane_in_kernel(parts):
    received = lax.all_to_all(parts, PLANE, 0, 0, tiled=False)
    (mine,) = call(plane_kernel, (), (received,), (shape(received.shape[1:], jnp.bfloat16),))
    return mine


def sum_plane(parts):
    received = lax.all_to_all(parts, PLANE, 0, 0, tiled=False)
    return jnp.sum(received.astype(jnp.float32), axis=0).astype(jnp.bfloat16)


def swap_depth(value, flip):
    depth = lax.axis_size("z")
    return lax.ppermute(value, "z", [(i, i ^ flip) for i in range(depth)])


def sum_depth(mine, beside=None):
    planes = lax.axis_size(PLANE)
    other, beside = lax.optimization_barrier((swap_depth(mine, 1), beside))
    pair = (mine.astype(jnp.float32) + other.astype(jnp.float32)).astype(jnp.bfloat16)
    (copies,) = call(
        replicate_kernel, (), (pair, swap_depth(pair, 3)), (shape((planes, *mine.shape), mine.dtype),)
    )
    return copies, beside


def spread_plane(copies):
    return lax.all_to_all(copies, PLANE, 0, 0, tiled=False)


def per_device(
    trunk_keys,
    trunk_values,
    trunk_rates,
    segment_end,
    fast_weights,
    step_sizes,
    branch_query,
    branch_keys,
    branch_values,
    branch_lengths,
    fork_points,
    out_gain,
):
    keys, values = trunk_keys[0], trunk_values[0]
    weights = fast_weights[:, 0]
    query, own_keys, own_values = branch_query[0], branch_keys[0], branch_values[0]
    rows, width = keys.shape
    hidden = weights.shape[1]
    planes = lax.axis_size(PLANE)
    trunk_total = rows * lax.axis_size(SEQ)
    total_width = width * lax.axis_size(HEAD)
    parts_shape = shape((planes, 3, hidden // planes, width), jnp.bfloat16)
    barrier = lax.optimization_barrier
    most, few = 11 * rows // 16, 5 * rows // 16

    keys_a = from_behind(own_keys[:most])
    parts = gradient_first(segment_end, trunk_rates, weights, keys, values, parts_shape)
    mine, keys_a = barrier((sum_plane_in_kernel(parts), keys_a))
    copies, _ = sum_depth(mine)
    copies, rest_keys, rest_values = barrier((copies, own_keys[most:], own_values[:few]))
    gathered, keys_b, values_b = barrier((spread_plane(copies), from_behind(rest_keys), from_behind(rest_values)))
    parts, state = update_and_gradient(
        segment_end, step_sizes, gathered, trunk_rates, weights, keys, values
    )
    parts, rest_values = barrier((parts, own_values[few:]))
    mine, values_c, query = barrier((sum_plane_in_kernel(parts), from_behind(rest_values), query))
    (attended,) = call(
        attend_kernel,
        (branch_lengths,),
        (query, own_keys, own_values, keys_a, keys_b, values_b, values_c),
        (shape((rows, width), jnp.float32),),
        flops=8 * rows * rows * width,
    )
    copies, attended = sum_depth(mine, attended)
    gathered = spread_plane(copies)
    total, energy, last = update_and_apply(
        segment_end, fork_points, step_sizes, gathered, weights, state, query, attended, trunk_total
    )
    energy = lax.psum(energy, HEAD)
    (result,) = call(
        functools.partial(last_kernel, width=total_width),
        (branch_lengths,),
        (total, energy, out_gain),
        (shape((rows, width), jnp.bfloat16),),
    )
    return (result[None], last[:, None])


def solution(mesh):
    fine = Mesh(mesh.devices.reshape(4, 4, 4, 2, 2), (*SEQ, *HEAD))
    rows = P(HEAD, SEQ, None)
    placed = (
        rows,
        rows,
        P(HEAD, SEQ),
        P(),
        P(None, HEAD, None, None),
        P(HEAD),
        rows,
        rows,
        rows,
        P(),
        P(),
        P(HEAD, None),
    )
    return jax.shard_map(
        per_device,
        mesh=fine,
        in_specs=placed,
        out_specs=(rows, P(None, HEAD, None, None)),
        check_vma=False,
    )
```

```python
import functools
import jax
import jax.numpy as jnp
from jax import lax
from jax.experimental import pallas as pl
from jax.experimental.pallas import tpu as pltpu
from jax.sharding import Mesh
from jax.sharding import PartitionSpec as P

PLANE = ("x", "y")
SEQ = ("x", "y", "z")
HEAD = ("w", "c")
NS_STEPS = 2
BR_SPAN = 4

poly_one = 3.4445
poly_two = -4.775
poly_three = 2.0315
VMEM_BYTES = 24 * 1024 * 1024
WHOLE_VMEM = 60 * 1024 * 1024
LAST_VMEM = 46 * 1024 * 1024
SECOND_VMEM = 61 * 1024 * 1024
CHUNK = 256
UPDATE_CHUNK = 512


def nt(left, right):
    return lax.dot_general(left, right, (((1,), (1,)), ((), ())), preferred_element_type=jnp.float32)


def nn(left, right):
    return jnp.dot(left, right, preferred_element_type=jnp.float32)


def column_of(row):
    return jnp.transpose(jnp.broadcast_to(row, (128, row.shape[1])))


def emit_gradient(weights, keys_ref, values_ref, rates, parts_ref, parts_hbm, sems, ready=lambda name: None):
    step = parts_ref.shape[2]
    sent = []
    rows, width = weights[0].shape
    ready("keys")
    keys = keys_ref[...]
    pushed = None
    for start in range(0, rows, CHUNK):
        cut = slice(start, start + CHUNK)
        if start == 0:
            ready("first")
        first = nt(weights[0][cut], keys)
        if start == 0:
            ready("third")
        third = nt(weights[1][cut], keys)
        gate = jax.nn.sigmoid(first)
        silu = first * gate
        hidden = (silu * third).astype(jnp.bfloat16)
        if start == 0:
            ready("rates")
            rate_columns = jnp.tile(column_of(rates()), (1, width // 128))
            ready("values")
            pushed = (rate_columns * values_ref[...].astype(jnp.float32)).astype(jnp.bfloat16)
            ready("second")
        returned = nt(weights[2][cut], pushed)
        delta_first = (returned * third * gate * (1.0 + first * (1.0 - gate))).astype(jnp.bfloat16)
        delta_third = (returned * silu).astype(jnp.bfloat16)
        for kind, grad in enumerate((nn(delta_first, keys), nn(delta_third, keys), nn(hidden, pushed))):
            grad = grad.astype(jnp.bfloat16)
            for part in range(CHUNK // step):
                parts_ref[start // step + part, kind] = grad[part * step : (part + 1) * step]
            slots = pl.ds(start // step, CHUNK // step)
            copy = pltpu.make_async_copy(
                parts_ref.at[slots, kind], parts_hbm.at[slots, kind], sems.at[len(sent)]
            )
            copy.start()
            sent.append(copy)
    for copy in sent:
        copy.wait()


def fetch_gathered(gathered_hbm, gathered_ref, sems):
    copies = [
        pltpu.make_async_copy(gathered_hbm.at[:, kind], gathered_ref.at[kind], sems.at[kind])
        for kind in range(gathered_ref.shape[0])
    ]
    for copy in copies:
        copy.start()
    return copies


def emit_update(load, old_ref, step_size, x_ref, gram_ref, out_ref, begin, ready):
    kinds, rows, width = out_ref.shape
    for kind in range(kinds):
        wide = load(kind).reshape(rows, width).astype(jnp.float32)
        square = jnp.sum(jnp.sum(wide * wide, axis=0, keepdims=True), axis=1, keepdims=True)
        inverse = 1.0 / (jnp.sqrt(square) + 1e-07)
        x_ref[0, kind] = (wide * inverse).astype(jnp.bfloat16)
    begin()
    for sweep in range(NS_STEPS):
        now, later = sweep % 2, (sweep + 1) % 2
        if sweep == NS_STEPS - 1:
            ready()
        for kind in range(kinds):
            full = x_ref[now, kind]
            gram_ref[kind] = nt(full, full).astype(jnp.bfloat16)
        for kind in range(kinds):
            full = x_ref[now, kind]
            gram = gram_ref[kind]
            for start in range(0, rows, UPDATE_CHUNK):
                cut = slice(start, start + UPDATE_CHUNK)
                own = gram[cut]
                poly = (poly_two * own.astype(jnp.float32) + poly_three * nn(own, gram)).astype(jnp.bfloat16)
                moved = (poly_one * full[cut].astype(jnp.float32) + nn(poly, full)).astype(jnp.bfloat16)
                if sweep < NS_STEPS - 1:
                    x_ref[later, kind, cut] = moved
                else:
                    old = old_ref[kind, cut].astype(jnp.float32)
                    new = old + step_size * moved.astype(jnp.float32)
                    old_mean = jnp.mean(old * old, axis=-1, keepdims=True) + 1e-06
                    new_mean = jnp.mean(new * new, axis=-1, keepdims=True) + 1e-06
                    out_ref[kind, cut] = (new * (jnp.sqrt(old_mean) * lax.rsqrt(new_mean))).astype(jnp.bfloat16)


def place_in_seq():
    return lax.axis_index(SEQ).astype(jnp.int32)


def masked_rates(rates, split_ref, period):
    count = rates.shape[1]
    positions = place_in_seq() * count + lax.broadcasted_iota(jnp.int32, rates.shape, 1)
    early = positions < split_ref[0]
    return jnp.where(early if period == 0 else jnp.logical_not(early), rates, 0.0)


def first_kernel(
    split_ref,
    rates_hbm,
    weights_hbm,
    keys_hbm,
    values_hbm,
    parts_hbm,
    rates,
    weights,
    keys,
    values,
    parts,
    sems,
    parts_sems,
):
    copies = {
        "keys": pltpu.make_async_copy(keys_hbm, keys, sems.at[0]),
        "first": pltpu.make_async_copy(weights_hbm.at[0], weights.at[0], sems.at[1]),
        "third": pltpu.make_async_copy(weights_hbm.at[1], weights.at[1], sems.at[2]),
        "values": pltpu.make_async_copy(values_hbm, values, sems.at[3]),
        "second": pltpu.make_async_copy(weights_hbm.at[2], weights.at[2], sems.at[4]),
        "rates": pltpu.make_async_copy(rates_hbm, rates, sems.at[5]),
    }
    for copy in copies.values():
        copy.start()
    kinds = [weights.at[kind] for kind in range(3)]
    emit_gradient(kinds, keys, values, lambda: masked_rates(rates[...], split_ref, 0), parts, parts_hbm, parts_sems, lambda name: copies[name].wait())


def second_kernel(
    split_ref,
    step_ref,
    rates_hbm,
    gathered_hbm,
    weights_hbm,
    keys_hbm,
    values_hbm,
    parts_hbm,
    state_hbm,
    rates,
    weights,
    keys,
    values,
    x_ref,
    gram_ref,
    state,
    gathered,
    parts,
    sems,
    gathered_sems,
    parts_sems,
):
    fetches = fetch_gathered(gathered_hbm, gathered, gathered_sems)
    fetch_weights = pltpu.make_async_copy(weights_hbm, weights, sems.at[0])
    fetch_keys = pltpu.make_async_copy(keys_hbm, keys, sems.at[1])
    fetch_values = pltpu.make_async_copy(values_hbm, values, sems.at[2])
    fetch_rates = pltpu.make_async_copy(rates_hbm, rates, sems.at[4])

    def begin():
        fetch_weights.start()
        fetch_keys.start()
        fetch_values.start()
        fetch_rates.start()

    def load(kind):
        fetches[kind].wait()
        return gathered[kind]

    emit_update(load, weights, step_ref[0], x_ref, gram_ref, state, begin, fetch_weights.wait)
    keep = pltpu.make_async_copy(state, state_hbm, sems.at[3])
    keep.start()
    fetch_keys.wait()
    fetch_values.wait()
    fetch_rates.wait()
    kinds = [state.at[kind] for kind in range(3)]
    emit_gradient(kinds, keys, values, lambda: masked_rates(rates[...], split_ref, 1), parts, parts_hbm, parts_sems)
    keep.wait()


def attend_kernel(
    length_ref, query_ref, keys_ref, values_ref, keys_a_ref, keys_b_ref, values_b_ref, values_c_ref, out_ref
):
    rows, width = query_ref.shape
    seq = place_in_seq()
    branch = seq // BR_SPAN
    place = seq % BR_SPAN
    live = length_ref[branch] - place * rows
    scale = width ** (-0.5)
    prior_keys = jnp.concatenate([keys_a_ref[...], keys_b_ref[...]], axis=0)
    prior_values = jnp.concatenate([values_b_ref[...], values_c_ref[...]], axis=0)
    chunk = 128
    for start in range(0, rows, chunk):
        cut = slice(start, start + chunk)
        query = query_ref[cut]
        row = start + lax.broadcasted_iota(jnp.int32, (chunk, rows), 0)
        slot = lax.broadcasted_iota(jnp.int32, (chunk, rows), 1)
        behind = slot > row
        allowed = (slot == row) | (slot < jnp.where(behind, jnp.where(place > 0, rows, 0), live))
        scores = jnp.where(behind, nt(query, prior_keys), nt(query, keys_ref[...])) * scale
        scores = jnp.where(allowed, scores, -1e30)
        top = jnp.max(scores, axis=-1, keepdims=True)
        power = jnp.exp(scores - top)
        share = power * (1.0 / jnp.sum(power, axis=-1, keepdims=True))
        out_ref[cut] = nn(jnp.where(behind, share, 0.0).astype(jnp.bfloat16), prior_values) + nn(
            jnp.where(behind, 0.0, share).astype(jnp.bfloat16), values_ref[...]
        )


def third_kernel(
    split_ref,
    fork_ref,
    step_ref,
    gathered_ref,
    attended_ref,
    weights_hbm,
    state_hbm,
    query_hbm,
    total_ref,
    energy_ref,
    last_hbm,
    old,
    query,
    x_ref,
    gram_ref,
    pool,
    sems,
    trunk_total,
):
    fork = fork_ref[place_in_seq() // BR_SPAN]
    early = fork < split_ref[0]
    final = jnp.logical_and(jnp.logical_not(early), fork >= trunk_total)
    fetch_old = pltpu.make_async_copy(state_hbm, old, sems.at[0])
    fetch_query = pltpu.make_async_copy(query_hbm, query, sems.at[1])
    fetch_first = pltpu.make_async_copy(weights_hbm, pool.at[1], sems.at[2])
    fetch_state = pltpu.make_async_copy(state_hbm, pool.at[1], sems.at[2])

    def begin():
        fetch_old.start()
        fetch_query.start()

        @pl.when(early)
        def _():
            fetch_first.start()

        @pl.when(jnp.logical_not(early))
        def _():
            fetch_state.start()

    emit_update(lambda kind: gathered_ref[:, kind], old, step_ref[0], x_ref, gram_ref, pool.at[0], begin, fetch_old.wait)
    keep = pltpu.make_async_copy(pool.at[0], last_hbm, sems.at[3])
    keep.start()
    fetch_query.wait()
    fetch_state.wait()
    pick = jnp.where(final, 0, 1)
    rows = query.shape[0]
    for start in range(0, rows, UPDATE_CHUNK):
        cut = slice(start, start + UPDATE_CHUNK)
        first = nt(query[cut], pool[pick, 0])
        third = nt(query[cut], pool[pick, 1])
        hidden = (first * jax.nn.sigmoid(first) * third).astype(jnp.bfloat16)
        total = attended_ref[cut] + nn(hidden, pool[pick, 2])
        total_ref[cut] = total
        energy = jnp.sum(total * total, axis=-1, keepdims=True)
        energy_ref[:, cut] = jnp.transpose(jnp.broadcast_to(energy, (UPDATE_CHUNK, 128)))[0:1]
    keep.wait()


def last_kernel(length_ref, total_ref, energy_ref, gain_ref, out_ref, width):
    rows = total_ref.shape[0]
    seq = place_in_seq()
    live = length_ref[seq // BR_SPAN] - (seq % BR_SPAN) * rows
    slot = lax.broadcasted_iota(jnp.int32, (1, rows), 1)
    inverse = jnp.where(slot < live, lax.rsqrt(energy_ref[...] / width + 1e-06), 0.0)
    columns = jnp.tile(column_of(inverse), (1, total_ref.shape[1] // 128))
    out_ref[...] = (total_ref[...] * columns * gain_ref[...]).astype(jnp.bfloat16)


def replicate_kernel(*refs):
    total = refs[0][...].astype(jnp.float32)
    for ref in refs[1:-1]:
        total = total + ref[...].astype(jnp.float32)
    total = total.astype(jnp.bfloat16)
    for slot in range(refs[-1].shape[0]):
        refs[-1][slot] = total


def plane_kernel(received_ref, mine_ref):
    mine_ref[...] = jnp.sum(received_ref[...].astype(jnp.float32), axis=0).astype(jnp.bfloat16)


SMEM = pl.BlockSpec(memory_space=pltpu.SMEM)
VMEM = pl.BlockSpec(memory_space=pltpu.VMEM)
HBM = pl.BlockSpec(memory_space=pltpu.HBM)


def call(kernel, scalars, arrays, outs, held=(), held_outs=(), scratch=(), flops=0, vmem=VMEM_BYTES):
    moved = sum(array.size * array.dtype.itemsize for array in (*arrays, *held, *outs, *held_outs))
    return pl.pallas_call(
        kernel,
        out_shape=(*outs, *held_outs),
        in_specs=[SMEM] * len(scalars) + [VMEM] * len(arrays) + [HBM] * len(held),
        out_specs=[VMEM] * len(outs) + [HBM] * len(held_outs),
        scratch_shapes=list(scratch),
        compiler_params=pltpu.CompilerParams(vmem_limit_bytes=vmem),
        cost_estimate=pl.CostEstimate(flops=flops, bytes_accessed=moved, transcendentals=0),
    )(*scalars, *arrays, *held)


def shape(dims, kind):
    return jax.ShapeDtypeStruct(dims, kind)


def space(dims, kind=jnp.bfloat16):
    return pltpu.VMEM(dims, kind)


def gradient_first(split, rates, weights, keys, values, parts_shape):
    scratch = (
        space(rates.shape, rates.dtype),
        space(weights.shape),
        space(keys.shape),
        space(values.shape),
        space(parts_shape.shape),
        pltpu.SemaphoreType.DMA((6,)),
        pltpu.SemaphoreType.DMA((3 * keys.shape[0] // CHUNK,)),
    )
    (parts,) = call(
        first_kernel,
        (split,),
        (),
        (),
        (rates, weights, keys, values),
        (parts_shape,),
        scratch,
        flops=12 * keys.size * weights.shape[1],
        vmem=WHOLE_VMEM,
    )
    return parts


def by_kind(gathered):
    planes, kinds, step, width = gathered.shape
    return space((kinds, planes, step, width))


def update_and_gradient(split, step, gathered, rates, weights, keys, values):
    full = weights.shape
    scratch = (
        space(rates.shape, rates.dtype),
        space(full),
        space(keys.shape),
        space(values.shape),
        space((2, *full)),
        space(full),
        space(full),
        by_kind(gathered),
        space(gathered.shape),
        pltpu.SemaphoreType.DMA((5,)),
        pltpu.SemaphoreType.DMA((3,)),
        pltpu.SemaphoreType.DMA((3 * full[1] // CHUNK,)),
    )
    return call(
        second_kernel,
        (split, step),
        (),
        (),
        (rates, gathered, weights, keys, values),
        (shape(gathered.shape, jnp.bfloat16), shape(full, jnp.bfloat16)),
        scratch,
        flops=48 * keys.size * full[1],
        vmem=SECOND_VMEM,
    )


def update_and_apply(split, forks, step, gathered, weights, state, query, attended, trunk_total):
    full = weights.shape
    rows, width = query.shape
    scratch = (
        space(full),
        space(query.shape),
        space((2, *full)),
        space(full),
        space((2, *full)),
        pltpu.SemaphoreType.DMA((4,)),
    )
    return call(
        functools.partial(third_kernel, trunk_total=trunk_total),
        (split, forks, step),
        (gathered, attended),
        (shape((rows, width), jnp.float32), shape((1, rows), jnp.float32)),
        (weights, state, query),
        (shape(full, jnp.bfloat16),),
        scratch,
        flops=42 * query.size * full[1],
        vmem=LAST_VMEM,
    )


def from_behind(value):
    count = lax.axis_size("z")
    return lax.ppermute(value, "z", [(source, source + 1) for source in range(count - 1)])


def sum_plane_in_kernel(parts):
    received = lax.all_to_all(parts, PLANE, 0, 0, tiled=False)
    (mine,) = call(plane_kernel, (), (received,), (shape(received.shape[1:], jnp.bfloat16),))
    return mine


def sum_plane(parts):
    received = lax.all_to_all(parts, PLANE, 0, 0, tiled=False)
    return jnp.sum(received.astype(jnp.float32), axis=0).astype(jnp.bfloat16)


def swap_depth(value, flip):
    depth = lax.axis_size("z")
    return lax.ppermute(value, "z", [(i, i ^ flip) for i in range(depth)])


def sum_depth(mine, beside=None):
    planes = lax.axis_size(PLANE)
    other, beside = lax.optimization_barrier((swap_depth(mine, 3), beside))
    pair = (mine.astype(jnp.float32) + other.astype(jnp.float32)).astype(jnp.bfloat16)
    (copies,) = call(
        replicate_kernel, (), (pair, swap_depth(pair, 1)), (shape((planes, *mine.shape), mine.dtype),)
    )
    return copies, beside


def spread_plane(copies):
    return lax.all_to_all(copies, PLANE, 0, 0, tiled=False)


def per_device(
    trunk_keys,
    trunk_values,
    trunk_rates,
    segment_end,
    fast_weights,
    step_sizes,
    branch_query,
    branch_keys,
    branch_values,
    branch_lengths,
    fork_points,
    out_gain,
):
    keys, values = trunk_keys[0], trunk_values[0]
    weights = fast_weights[:, 0]
    query, own_keys, own_values = branch_query[0], branch_keys[0], branch_values[0]
    rows, width = keys.shape
    hidden = weights.shape[1]
    planes = lax.axis_size(PLANE)
    trunk_total = rows * lax.axis_size(SEQ)
    total_width = width * lax.axis_size(HEAD)
    parts_shape = shape((planes, 3, hidden // planes, width), jnp.bfloat16)
    barrier = lax.optimization_barrier
    most, few = 11 * rows // 16, 5 * rows // 16

    keys_a = from_behind(own_keys[:most])
    parts = gradient_first(segment_end, trunk_rates, weights, keys, values, parts_shape)
    mine, keys_a = barrier((sum_plane_in_kernel(parts), keys_a))
    copies, _ = sum_depth(mine)
    copies, rest_keys, rest_values = barrier((copies, own_keys[most:], own_values[:few]))
    gathered, keys_b, values_b = barrier((spread_plane(copies), from_behind(rest_keys), from_behind(rest_values)))
    parts, state = update_and_gradient(
        segment_end, step_sizes, gathered, trunk_rates, weights, keys, values
    )
    parts, rest_values = barrier((parts, own_values[few:]))
    mine, values_c, query = barrier((sum_plane_in_kernel(parts), from_behind(rest_values), query))
    (attended,) = call(
        attend_kernel,
        (branch_lengths,),
        (query, own_keys, own_values, keys_a, keys_b, values_b, values_c),
        (shape((rows, width), jnp.float32),),
        flops=8 * rows * rows * width,
    )
    copies, attended = sum_depth(mine, attended)
    gathered = spread_plane(copies)
    total, energy, last = update_and_apply(
        segment_end, fork_points, step_sizes, gathered, weights, state, query, attended, trunk_total
    )
    energy = lax.psum(energy, HEAD)
    (result,) = call(
        functools.partial(last_kernel, width=total_width),
        (branch_lengths,),
        (total, energy, out_gain),
        (shape((rows, width), jnp.bfloat16),),
    )
    return (result[None], last[:, None])


def solution(mesh):
    fine = Mesh(mesh.devices.reshape(4, 4, 4, 2, 2), (*SEQ, *HEAD))
    rows = P(HEAD, SEQ, None)
    placed = (
        rows,
        rows,
        P(HEAD, SEQ),
        P(),
        P(None, HEAD, None, None),
        P(HEAD),
        rows,
        rows,
        rows,
        P(),
        P(),
        P(HEAD, None),
    )
    return jax.shard_map(
        per_device,
        mesh=fine,
        in_specs=placed,
        out_specs=(rows, P(None, HEAD, None, None)),
        check_vma=False,
    )
```
